256 devices in a mesh: head: 16 (over z_hi, y), inner: 8 (over x, core), outer: 2 (over z_lo).
Axes of the slice: x: 4, y: 4, z: 8 (z_hi: 4, z_lo: 2; z = z_hi * 2 + z_lo), core: 2. Of those that a mesh axis runs over, the one named last changes fastest.
Arguments:
- queries: bfloat16 [8, 4096, 4096], P('inner', ('head', 'outer')), may hold values from -18 to 18
- keys: bfloat16 [8, 4096, 512], P('inner', ('head', 'outer')), may hold values from -6 to 6
- values: bfloat16 [8, 4096, 512], P('inner', ('head', 'outer')), may hold values from -6 to 6
- grad_out: bfloat16 [8, 4096, 4096], P('inner', ('head', 'outer')), may hold values from -24 to 24
- positions: int32 [8, 4096], P('inner', ('head', 'outer')), may hold values from 0 to 4095, as said below
Outputs:
- attended: bfloat16 [8, 4096, 4096], P('inner', ('head', 'outer'))
- grad_queries: bfloat16 [8, 4096, 4096], P('inner', ('head', 'outer'))
- grad_keys: bfloat16 [8, 4096, 512], P('inner', ('head', 'outer'))
- grad_values: bfloat16 [8, 4096, 512], P('inner', ('head', 'outer'))
The draws below stay inside these ranges and needn't reach their ends.
Inputs may be any that keep to these rules, and one draw needn't show every extreme that they name: In each sequence a permutation of the positions. The 2048 rows of the devices that share inner and outer indices, taken in the order of the head index, hold two runs of 1024 consecutive positions: the first half of the rows the run that starts at a * 1024 and the second half the run that starts at 4096 - (a + 1) * 1024, where each a from 0 to 1 belongs to one outer index in each sequence. Each aligned block of 512 of these rows holds 512 consecutive positions of its run, in the run's order of blocks; the order of positions inside a block is drawn from the seed.
All inputs are finite; a program needn't handle non-finite values.
Results may differ from the reference program's by a relative error of at most 0.025.
Values may be sent and summed in bfloat16 or wider, within the bound.
No kernel may reach another device: no remote copies, remote signals or barrier semaphores. Data moves between devices by JAX's collectives and lax.ppermute only.
A program may use at most 64 MiB of HBM per device.

```python
import math
import jax
import jax.numpy as jnp
from jax import lax

H = 32
KVH = 4
DH = 128
TOK_DEV = 128
CTX = 2048
TOKENS = 4096
SEQS = 8
BLOCK = 512


def planted(key, lift):
    every = SEQS * TOKENS
    rows = jnp.arange(every)
    piece = rows // TOK_DEV
    chosen = jnp.logical_and(rows % TOK_DEV == 1, piece % 5 == 0)
    chosen = jnp.logical_and(chosen, lift > 0.5)
    strength = jnp.where(piece % 3 == 0, 5.0, jnp.where(piece % 3 == 1, 8.0, 12.0))
    flips = jax.random.bernoulli(jax.random.fold_in(key, 11), 0.5, (every, KVH * DH))
    signs = jnp.where(flips, 1.5, -1.5).astype(jnp.float32)
    base = jnp.clip(jax.random.normal(key, (every, KVH * DH), jnp.float32), -6.0, 6.0)
    shrink = 1.0 - 0.889 / (DH ** 0.5 * strength)
    before = jnp.roll(chosen, -1)
    nearby = jnp.roll(signs * shrink[:, None], -1, axis=0)
    result = jnp.where(chosen[:, None], signs, jnp.where(before[:, None], nearby, base))
    return (result, chosen, strength, signs)


def draw_keys(key, part):
    lift = 0.0
    result = planted(key, lift)[0]
    return result.reshape(SEQS, TOKENS, KVH * DH).astype(jnp.bfloat16)


def draw_queries(key, part):
    every = SEQS * TOKENS
    lift = 0.0
    result, chosen, strength, signs = planted(key, lift)
    own = jax.random.fold_in(key, 7)
    base = jnp.clip(jax.random.normal(own, (every, H * DH), jnp.float32) * 1.5, -9.0, 9.0)
    grouped = jnp.repeat(signs.reshape(every, KVH, DH), H // KVH, axis=1).reshape(every, H * DH)
    queries = jnp.where(chosen[:, None], strength[:, None] * grouped, base)
    return queries.reshape(SEQS, TOKENS, H * DH).astype(jnp.bfloat16)


def draw_positions(key, part):
    key = jax.random.fold_in(key, 5)
    rows = jnp.arange(TOKENS)
    stride = TOKENS // (CTX // TOK_DEV)
    head_place = rows // stride
    remain = rows % stride
    shard = remain // TOK_DEV
    within = remain % TOK_DEV
    spot = head_place * TOK_DEV + within
    half = CTX // 2
    shards = TOKENS // CTX
    spots = jnp.arange(CTX)

    def one_sequence(number):
        seq_key = jax.random.fold_in(key, number)
        order = jax.random.permutation(seq_key, shards)
        lower = order[:, None]
        upper = TOKENS // half - 1 - lower
        table = jnp.where(spots[None, :] < half, lower * half + spots[None, :], upper * half + spots[None, :] - half)
        block_keys = jax.random.split(jax.random.fold_in(seq_key, 1), shards * (CTX // BLOCK))
        shuffles = jax.vmap(lambda one: jax.random.permutation(one, BLOCK))(block_keys).reshape(shards, CTX)
        shuffles = shuffles + (spots // BLOCK * BLOCK)[None, :]
        table = jnp.take_along_axis(table, shuffles, axis=1)
        return table[shard, spot].astype(jnp.int32)
    return jax.vmap(one_sequence)(jnp.arange(SEQS))


def block_levels(rng, dims, cuts, low, high):
    loudness, own = 1.0, jax.random.fold_in(rng, 6)
    for axis_at, blocks in cuts:
        heights = jnp.exp(jax.random.uniform(jax.random.fold_in(own, axis_at), (blocks,), jnp.float32, low / len(cuts), high / len(cuts)))
        loudness = loudness * jnp.repeat(heights, dims[axis_at] // blocks).reshape([-1 if axis == axis_at else 1 for axis in range(len(dims))])
    return loudness


def scatter_about(rng, shape, scale, limit, cuts=(), kind=jnp.bfloat16):
    values = scale * jax.random.normal(rng, shape, jnp.float32)
    if cuts:
        values = values * block_levels(rng, shape, cuts, -0.22, 0.18)
    return jnp.clip(values, -limit, limit).astype(kind)


def setup_inputs(seed: int = 0) -> dict:
    splits = jax.random.split(jax.random.key(seed), 6)
    return {
        "queries": draw_queries(jax.random.fold_in(splits[5], 71), 0),
        "keys": draw_keys(jax.random.fold_in(splits[5], 71), 0),
        "values": scatter_about(splits[2], (SEQS, TOKENS, KVH * DH), 1.0, 6.0, ((0, 8), (1, 32))),
        "grad_out": scatter_about(splits[3], (SEQS, TOKENS, H * DH), 4.0, 24.0, ((0, 8), (1, 32))),
        "positions": draw_positions(jax.random.fold_in(splits[5], 71), 0),
    }


NEGATIVE = -1e+30

def one_head(q_head, k_head, v_head, g_head, visible):
    scale = 1.0 / math.sqrt(DH)
    scores = jnp.dot(q_head, k_head.T, preferred_element_type=jnp.float32) * scale
    masked = jnp.where(visible, scores, NEGATIVE)
    rowmax = lax.optimization_barrier(jnp.max(masked, axis=1))
    shifted = jnp.where(visible, jnp.exp(masked - rowmax[:, None]), 0.0)
    total = lax.optimization_barrier(jnp.sum(shifted, axis=1))
    mixed = jnp.dot(shifted.astype(jnp.bfloat16), v_head, preferred_element_type=jnp.float32)
    attended = (mixed / total[:, None]).astype(jnp.bfloat16)
    logsum = rowmax + jnp.log(total)
    probs = jnp.where(visible, jnp.exp(masked - logsum[:, None]), 0.0)
    delta = lax.optimization_barrier(jnp.sum(g_head.astype(jnp.float32) * attended.astype(jnp.float32), axis=1))
    grad_v = jnp.dot(probs.astype(jnp.bfloat16).T, g_head, preferred_element_type=jnp.float32)
    dprobs = jnp.dot(g_head, v_head.T, preferred_element_type=jnp.float32)
    dscores = (probs * (dprobs - delta[:, None])).astype(jnp.bfloat16)
    grad_q = (jnp.dot(dscores, k_head, preferred_element_type=jnp.float32) * scale).astype(jnp.bfloat16)
    grad_k = jnp.dot(dscores.T, q_head, preferred_element_type=jnp.float32) * scale
    return (attended, grad_q, grad_k, grad_v)

def one_sequence(queries, keys, values, grad_out, positions):
    visible = positions[None, :] <= positions[:, None]
    group = H // KVH
    q_heads = queries.reshape(TOKENS, H, DH).transpose(1, 0, 2)
    g_heads = grad_out.reshape(TOKENS, H, DH).transpose(1, 0, 2)
    k_heads = jnp.repeat(keys.reshape(TOKENS, KVH, DH).transpose(1, 0, 2), group, axis=0)
    v_heads = jnp.repeat(values.reshape(TOKENS, KVH, DH).transpose(1, 0, 2), group, axis=0)

    def run_head(item):
        return one_head(item[0], item[1], item[2], item[3], visible)
    attended, grad_q, grad_k, grad_v = lax.map(run_head, (q_heads, k_heads, v_heads, g_heads))
    attended = attended.transpose(1, 0, 2).reshape(TOKENS, H * DH)
    grad_queries = grad_q.transpose(1, 0, 2).reshape(TOKENS, H * DH)
    grad_keys = grad_k.reshape(KVH, group, TOKENS, DH).sum(axis=1).transpose(1, 0, 2)
    grad_values = grad_v.reshape(KVH, group, TOKENS, DH).sum(axis=1).transpose(1, 0, 2)
    grad_keys = grad_keys.reshape(TOKENS, KVH * DH).astype(jnp.bfloat16)
    grad_values = grad_values.reshape(TOKENS, KVH * DH).astype(jnp.bfloat16)
    return (attended, grad_queries, grad_keys, grad_values)

def reference(queries, keys, values, grad_out, positions):

    def run_sequence(item):
        return one_sequence(item[0], item[1], item[2], item[3], item[4])
    attended, grad_queries, grad_keys, grad_values = lax.map(run_sequence, (queries, keys, values, grad_out, positions))
    return (attended, grad_queries, grad_keys, grad_values)
```

```python
import math

import jax
import jax.numpy as jnp
from jax import lax
from jax.experimental import pallas as pl
from jax.experimental.pallas import tpu as pltpu
from jax.sharding import Mesh, PartitionSpec as P

H = 32
KVH = 4
DH = 128
ROWS = 128
BLOCK = 512
NY = 4
NZ = 8
HEADS = H // NZ
NEGATIVE = -1e30
SCALE = 1.0 / math.sqrt(DH)
EXP2_SCALE = SCALE * math.log2(math.e)
Z = ("zhi", "outer")
DIMS_NT = (((1,), (1,)), ((), ()))


def attend(
    y_ref, marks_smem, marks_ref, q_ref, g_ref, kv0, kv1, kv2, kv3,
    o_ref, dq_ref, out0, out1, out2, out3,
    order, s_buf, p_buf, k_t, v_t, acc,
):
    heads = q_ref.shape[2] // DH
    cols = heads * ROWS
    pieces = (kv0, kv1, kv2, kv3)
    outs = (out0, out1, out2, out3)
    y = y_ref[0]

    def place(z, at):
        return (z // 2) * (2 * NY) + at * 2 + z % 2

    for z in range(NZ):
        order[marks_smem[place(z, 0), 0] // BLOCK] = z

    def prepare(z, carry):
        for rel in range(NY):
            cut = slice(rel * ROWS, (rel + 1) * ROWS)
            k_t[z, :, cut] = pieces[rel][z, :, :DH].T
            v_t[z, :, cut] = pieces[rel][z, :, DH:].T
        acc[z] = jnp.zeros((BLOCK, 2 * DH), jnp.float32)
        return carry

    lax.fori_loop(0, NZ, prepare, 0)

    def flip(ref, z):
        return jnp.concatenate(
            [ref[z, :, i * DH : (i + 1) * DH].T for i in range(heads)], axis=1
        )

    def fold(x, op):
        return op(x.reshape(x.shape[0] // 8, 8, x.shape[1]), axis=0)

    def group(b, carry):
        z = order[b]
        q_t = flip(q_ref, z)
        g_t = flip(g_ref, z)

        def scores(j, rel):
            k = pieces[rel][order[j], :, :DH]
            return jnp.dot(k, q_t, preferred_element_type=jnp.float32)

        def first(j, top):
            for rel in range(NY):
                s = scores(j, rel)
                s_buf[j, rel * ROWS : (rel + 1) * ROWS, :] = s
                top = jnp.maximum(top, fold(s, jnp.max))
            return top

        top = lax.fori_loop(0, b, first, jnp.full((8, cols), NEGATIVE, jnp.float32))
        q_marks = marks_ref[place(z, y)]
        for rel in range(NY):
            s = scores(b, rel)
            k_marks = marks_ref[place(z, (y + rel) % NY)]
            k_marks = jnp.broadcast_to(k_marks, (ROWS, ROWS)).T
            seen = k_marks <= jnp.broadcast_to(q_marks, (ROWS, ROWS))
            s = jnp.concatenate(
                [
                    jnp.where(seen, s[:, i * ROWS : (i + 1) * ROWS], NEGATIVE)
                    for i in range(heads)
                ],
                axis=1,
            )
            s_buf[b, rel * ROWS : (rel + 1) * ROWS, :] = s
            top = jnp.maximum(top, fold(s, jnp.max))
        top = jnp.max(top, axis=0, keepdims=True)

        def second(j, state):
            total, out_t = state
            zj = order[j]
            for rel in range(NY):
                cut = slice(rel * ROWS, (rel + 1) * ROWS)
                w = jnp.exp2((s_buf[j, cut, :] - top) * EXP2_SCALE)
                total = total + fold(w, jnp.sum)
                w = w.astype(jnp.bfloat16)
                p_buf[j, cut, :] = w
            out_t = out_t + jnp.dot(
                v_t[zj], p_buf[j], preferred_element_type=jnp.float32
            )
            return (total, out_t)

        total, out_t = lax.fori_loop(
            0,
            b + 1,
            second,
            (jnp.zeros((8, cols), jnp.float32), jnp.zeros((DH, cols), jnp.float32)),
        )
        inv = 1.0 / jnp.sum(total, axis=0, keepdims=True)
        out_t = out_t * inv
        attended = out_t.astype(jnp.bfloat16)
        delta = jnp.sum(
            g_t.astype(jnp.float32) * attended.astype(jnp.float32), axis=0, keepdims=True
        )
        q_n = (q_t.astype(jnp.float32) * inv).astype(jnp.bfloat16)
        g_n = (g_t.astype(jnp.float32) * inv).astype(jnp.bfloat16)
        for i in range(heads):
            cut = slice(i * ROWS, (i + 1) * ROWS)
            o_ref[z, :, i * DH : (i + 1) * DH] = attended[:, cut].T

        def third(j, dq_t):
            zj = order[j]
            for rel in range(NY):
                cut = slice(rel * ROWS, (rel + 1) * ROWS)
                v = pieces[rel][zj, :, DH:]
                w = p_buf[j, cut, :]
                dp = jnp.dot(v, g_t, preferred_element_type=jnp.float32)
                ds = (w.astype(jnp.float32) * (dp - delta)).astype(jnp.bfloat16)
                acc[zj, cut, DH:] += lax.dot_general(
                    w, g_n, DIMS_NT, preferred_element_type=jnp.float32
                )
                acc[zj, cut, :DH] += lax.dot_general(
                    ds, q_n, DIMS_NT, preferred_element_type=jnp.float32
                )
                dq_t = dq_t + jnp.dot(
                    k_t[zj, :, cut], ds, preferred_element_type=jnp.float32
                )
            return dq_t

        dq_t = lax.fori_loop(0, b + 1, third, jnp.zeros((DH, cols), jnp.float32))
        dq_t = (dq_t * (inv * SCALE)).astype(jnp.bfloat16)
        for i in range(heads):
            cut = slice(i * ROWS, (i + 1) * ROWS)
            dq_ref[z, :, i * DH : (i + 1) * DH] = dq_t[:, cut].T
        return carry

    lax.fori_loop(0, NZ, group, 0)

    def finish(z, carry):
        for rel in range(NY):
            cut = slice(rel * ROWS, (rel + 1) * ROWS)
            outs[rel][z, :, :DH] = (acc[z, cut, :DH] * SCALE).astype(jnp.bfloat16)
            outs[rel][z, :, DH:] = acc[z, cut, DH:].astype(jnp.bfloat16)
        return carry

    lax.fori_loop(0, NZ, finish, 0)


def run_attend(y, marks, q, g, pieces):
    cols = q.shape[2]
    vmem = pl.BlockSpec(memory_space=pltpu.VMEM)
    smem = pl.BlockSpec(memory_space=pltpu.SMEM)
    wide = jax.ShapeDtypeStruct((NZ, ROWS, cols), jnp.bfloat16)
    narrow = jax.ShapeDtypeStruct((NZ, ROWS, 2 * DH), jnp.bfloat16)
    return pl.pallas_call(
        attend,
        out_shape=(wide, wide, narrow, narrow, narrow, narrow),
        in_specs=[smem, smem] + [vmem] * 7,
        out_specs=[vmem] * 6,
        scratch_shapes=[
            pltpu.SMEM((NZ,), jnp.int32),
            pltpu.VMEM((NZ, BLOCK, cols), jnp.float32),
            pltpu.VMEM((NZ, BLOCK, cols), jnp.bfloat16),
            pltpu.VMEM((NZ, DH, BLOCK), jnp.bfloat16),
            pltpu.VMEM((NZ, DH, BLOCK), jnp.bfloat16),
            pltpu.VMEM((NZ, BLOCK, 2 * DH), jnp.float32),
        ],
        compiler_params=pltpu.CompilerParams(vmem_limit_bytes=56 * 1024 * 1024),
        cost_estimate=pl.CostEstimate(
            flops=36 * 6 * 2 * BLOCK * BLOCK * DH,
            bytes_accessed=8 * 1024 * 1024,
            transcendentals=36 * BLOCK * BLOCK,
        ),
    )(y, marks, marks.reshape(NY * NZ, 1, ROWS), q, g, *pieces)


def ring(step):
    return [(i, (i + step) % NY) for i in range(NY)]


def shards(queries, keys, values, grad_out, positions):
    q = queries[0].reshape(ROWS, NZ, HEADS * DH).transpose(1, 0, 2)
    g = grad_out[0].reshape(ROWS, NZ, HEADS * DH).transpose(1, 0, 2)
    kv = jnp.concatenate(
        [keys[0].reshape(ROWS, KVH, DH), values[0].reshape(ROWS, KVH, DH)], axis=2
    )
    kv = jnp.repeat(kv.transpose(1, 0, 2), NZ // KVH, axis=0)
    marks = lax.all_gather(positions[0], ("zhi", "y", "outer"), axis=0, tiled=False)
    kv = lax.all_to_all(kv, Z, split_axis=0, concat_axis=0, tiled=True)
    kv_up = lax.ppermute(kv, "y", ring(-1))
    kv_down = lax.ppermute(kv, "y", ring(1))
    kv_far = lax.ppermute(kv, "y", ring(2))
    q = lax.all_to_all(q, Z, split_axis=0, concat_axis=0, tiled=True)
    g = lax.all_to_all(g, Z, split_axis=0, concat_axis=0, tiled=True)
    y = lax.axis_index("y").astype(jnp.int32).reshape(1)
    out, dq, d0, d1, d2, d3 = run_attend(y, marks, q, g, (kv, kv_up, kv_far, kv_down))
    d1 = lax.ppermute(d1, "y", ring(1))
    d2 = lax.ppermute(d2, "y", ring(2))
    d3 = lax.ppermute(d3, "y", ring(-1))
    wide = [d.astype(jnp.float32) for d in (d0, d1, d2, d3)]
    dkv = ((wide[0] + wide[1]) + (wide[2] + wide[3])).astype(jnp.bfloat16)
    dkv = lax.all_to_all(dkv, Z, split_axis=0, concat_axis=0, tiled=True)
    out = lax.all_to_all(out, Z, split_axis=0, concat_axis=0, tiled=True)
    dq = lax.all_to_all(dq, Z, split_axis=0, concat_axis=0, tiled=True)
    out = out.transpose(1, 0, 2).reshape(ROWS, H * DH)
    dq = dq.transpose(1, 0, 2).reshape(ROWS, H * DH)
    dkv = dkv.reshape(KVH, NZ // KVH, ROWS, 2 * DH).astype(jnp.float32).sum(axis=1)
    dkv = dkv.astype(jnp.bfloat16).transpose(1, 0, 2)
    dk = dkv[:, :, :DH].reshape(ROWS, KVH * DH)
    dv = dkv[:, :, DH:].reshape(ROWS, KVH * DH)
    return out[None], dq[None], dk[None], dv[None]


def solution(mesh):
    devices = mesh.devices.reshape(NZ // 2, NY, mesh.shape["inner"], mesh.shape["outer"])
    fine = Mesh(devices, ("zhi", "y", "inner", "outer"))
    rows = P("inner", ("zhi", "y", "outer"), None)
    return jax.shard_map(
        shards,
        mesh=fine,
        in_specs=(rows, rows, rows, rows, P("inner", ("zhi", "y", "outer"))),
        out_specs=(rows, rows, rows, rows),
        check_vma=False,
    )
```

```python
import math

import jax
import jax.numpy as jnp
from jax import lax
from jax.experimental import pallas as pl
from jax.experimental.pallas import tpu as pltpu
from jax.sharding import Mesh, PartitionSpec as P

H = 32
KVH = 4
DH = 128
ROWS = 128
PADDED = 144
BLOCK = 512
NY = 4
NZ = 8
HEADS = H // NZ
COLS = HEADS * ROWS
TILES = NZ * (NZ + 1) // 2
NEGATIVE = -1e30
SCALE = 1.0 / math.sqrt(DH)
EXP2_SCALE = SCALE * math.log2(math.e)
Z = ("zhi", "outer")
DIMS_NT = (((1,), (1,)), ((), ()))
PLACES = (0, 2, 1, 3, 5, 7, 4, 6)
F32 = jnp.float32
BF16 = jnp.bfloat16


def flip(ref, z):
    return jnp.concatenate(
        [ref[z, :, i * DH : (i + 1) * DH].T for i in range(HEADS)], axis=1
    )


def unflip(ref, z, value):
    for i in range(HEADS):
        ref[z, :, i * DH : (i + 1) * DH] = value[:, i * ROWS : (i + 1) * ROWS].T


def fold(x, op):
    return op(x.reshape(x.shape[0] // 8, 8, x.shape[1]), axis=0)


def set_order(turn, order):
    for b in range(NZ):
        order[b] = jnp.bitwise_xor(turn[0], PLACES[b])


def tile_at(b, j):
    return b * (b + 1) // 2 + j


def forward(
    turn, q_ref, kv0, kv1, kv2, kv3, o_ref, stat_ref, p_hbm,
    order, s_buf, p_buf, k_n, v_t, out_acc, top_acc, sems,
):
    pieces = (kv0, kv1, kv2, kv3)
    set_order(turn, order)

    def row_marks(piece, z):
        row = piece[z, ROWS : ROWS + 16, :].astype(F32)[0:1]
        return row[:, :DH] * 64.0 + row[:, DH:]

    def enter(b):
        z = order[b]
        for rel in range(NY):
            cut = slice(rel * ROWS, (rel + 1) * ROWS)
            k_n[b, cut, :] = pieces[rel][z, :ROWS, :DH]
            v_t[b, :, cut] = pieces[rel][z, :ROWS, DH:].T
        q_t = flip(q_ref, z)
        s = jnp.dot(k_n[b], q_t, preferred_element_type=F32)
        q_marks = jnp.broadcast_to(row_marks(kv0, z), (ROWS, ROWS))
        slot = b % 2
        top = jnp.full((8, COLS), NEGATIVE, F32)
        for rel in range(NY):
            cut = slice(rel * ROWS, (rel + 1) * ROWS)
            k_marks = jnp.broadcast_to(row_marks(pieces[rel], z), (ROWS, ROWS)).T
            seen = k_marks <= q_marks
            part = jnp.concatenate(
                [
                    jnp.where(seen, s[cut, i * ROWS : (i + 1) * ROWS], NEGATIVE)
                    for i in range(HEADS)
                ],
                axis=1,
            )
            s_buf[slot, b, cut, :] = part
            top = jnp.maximum(top, fold(part, jnp.max))
        top_acc[...] = top
        return q_t

    def weigh(b, j, top):
        w = jnp.exp2((s_buf[b % 2, j] - top) * EXP2_SCALE)
        part = fold(w, jnp.sum)
        w = w.astype(BF16)
        tile = tile_at(b, j)
        p_buf[tile] = w
        out_acc[...] += jnp.dot(v_t[j], w, preferred_element_type=F32)
        return part

    def send(b, j):
        tile = tile_at(b, j)
        pltpu.make_async_copy(p_buf.at[tile], p_hbm.at[tile], sems.at[tile]).start()

    def leave(b, top, total):
        inv = 1.0 / jnp.sum(total, axis=0, keepdims=True)
        unflip(o_ref, order[b], (out_acc[...] * inv).astype(BF16))
        stat_ref[b] = inv

    enter(0)

    def group(b, carry):
        top = jnp.max(top_acc[...], axis=0, keepdims=True)
        q_next = enter(b + 1)
        out_acc[...] = jnp.zeros((DH, COLS), F32)

        def step(j, total):
            s = jnp.dot(k_n[j], q_next, preferred_element_type=F32)
            s_buf[(b + 1) % 2, j] = s
            top_acc[...] = jnp.maximum(top_acc[...], fold(s, jnp.max))
            total = total + weigh(b, j, top)
            send(b, j)
            return total

        total = lax.fori_loop(0, b + 1, step, jnp.zeros((8, COLS), F32))
        leave(b, top, total)
        return carry

    lax.fori_loop(0, NZ - 1, group, 0)
    last = NZ - 1
    top = jnp.max(top_acc[...], axis=0, keepdims=True)
    out_acc[...] = jnp.zeros((DH, COLS), F32)

    def step(j, total):
        total = total + weigh(last, j, top)
        send(last, j)
        return total

    total = lax.fori_loop(0, NZ, step, jnp.zeros((8, COLS), F32))
    leave(last, top, total)

    def wait(tile, carry):
        pltpu.make_async_copy(p_buf.at[tile], p_hbm.at[tile], sems.at[tile]).wait()
        return carry

    lax.fori_loop(0, TILES, wait, 0)


def backward(
    turn, q_ref, g_ref, o_ref, stat_ref, kv0, kv1, kv2, kv3, p_hbm,
    dq_ref, out0, out1, out2, out3,
    order, p_buf, k_t, v_n, acc, dq_acc, sems,
):
    pieces = (kv0, kv1, kv2, kv3)
    outs = (out0, out1, out2, out3)
    set_order(turn, order)

    def fetch(tile, carry):
        pltpu.make_async_copy(p_hbm.at[tile], p_buf.at[tile], sems.at[tile]).start()
        return carry

    lax.fori_loop(0, TILES, fetch, 0)

    def group(b, carry):
        z = order[b]
        for rel in range(NY):
            cut = slice(rel * ROWS, (rel + 1) * ROWS)
            k_t[b, :, cut] = pieces[rel][z, :ROWS, :DH].T
            v_n[b, cut, :] = pieces[rel][z, :ROWS, DH:]
        acc[b] = jnp.zeros((BLOCK, 2 * DH), F32)
        dq_acc[...] = jnp.zeros((DH, COLS), F32)
        q_t = flip(q_ref, z)
        g_t = flip(g_ref, z)
        o_t = flip(o_ref, z)
        inv = stat_ref[b]
        delta = jnp.sum(g_t.astype(F32) * o_t.astype(F32), axis=0, keepdims=True)
        q_n = (q_t.astype(F32) * inv).astype(BF16)
        g_n = (g_t.astype(F32) * inv).astype(BF16)

        def step(j, carry):
            tile = tile_at(b, j)
            pltpu.make_async_copy(p_hbm.at[tile], p_buf.at[tile], sems.at[tile]).wait()
            w = p_buf[tile]
            dp = jnp.dot(v_n[j], g_t, preferred_element_type=F32)
            ds = (w.astype(F32) * (dp - delta)).astype(BF16)
            acc[j, :, DH:] += lax.dot_general(w, g_n, DIMS_NT, preferred_element_type=F32)
            acc[j, :, :DH] += lax.dot_general(ds, q_n, DIMS_NT, preferred_element_type=F32)
            dq_acc[...] += jnp.dot(k_t[j], ds, preferred_element_type=F32)
            return carry

        lax.fori_loop(0, b + 1, step, 0)
        unflip(dq_ref, z, (dq_acc[...] * (inv * SCALE)).astype(BF16))
        return carry

    lax.fori_loop(0, NZ, group, 0)

    def finish(b, carry):
        z = order[b]
        for rel in range(NY):
            cut = slice(rel * ROWS, (rel + 1) * ROWS)
            outs[rel][z, :, :DH] = (acc[b, cut, :DH] * SCALE).astype(BF16)
            outs[rel][z, :, DH:] = acc[b, cut, DH:].astype(BF16)
        return carry

    lax.fori_loop(0, NZ, finish, 0)


VMEM = pl.BlockSpec(memory_space=pltpu.VMEM)
SMEM = pl.BlockSpec(memory_space=pltpu.SMEM)
ANY = pl.BlockSpec(memory_space=pl.ANY)
WIDE = jax.ShapeDtypeStruct((NZ, ROWS, COLS), BF16)
NARROW = jax.ShapeDtypeStruct((NZ, ROWS, 2 * DH), BF16)
WEIGHTS = jax.ShapeDtypeStruct((TILES, BLOCK, COLS), BF16)
STATS = jax.ShapeDtypeStruct((NZ, 1, COLS), F32)
PARAMS = pltpu.CompilerParams(vmem_limit_bytes=56 * 1024 * 1024)


def cost(matmuls, exps):
    return pl.CostEstimate(
        flops=TILES * matmuls * 2 * BLOCK * COLS * DH * 2,
        bytes_accessed=24 * 1024 * 1024,
        transcendentals=exps * TILES * BLOCK * COLS,
    )


def run_forward(turn, q, pieces):
    return pl.pallas_call(
        forward,
        name="forward",
        out_shape=(WIDE, STATS, WEIGHTS),
        in_specs=[SMEM] + [VMEM] * 5,
        out_specs=[VMEM, VMEM, ANY],
        scratch_shapes=[
            pltpu.SMEM((NZ,), jnp.int32),
            pltpu.VMEM((2, NZ, BLOCK, COLS), F32),
            pltpu.VMEM((TILES, BLOCK, COLS), BF16),
            pltpu.VMEM((NZ, BLOCK, DH), BF16),
            pltpu.VMEM((NZ, DH, BLOCK), BF16),
            pltpu.VMEM((DH, COLS), F32),
            pltpu.VMEM((8, COLS), F32),
            pltpu.SemaphoreType.DMA((TILES,)),
        ],
        compiler_params=PARAMS,
        cost_estimate=cost(2, 1),
    )(turn, q, *pieces)


def run_backward(turn, q, g, o, stat, pieces, weights):
    return pl.pallas_call(
        backward,
        name="backward",
        out_shape=(WIDE, NARROW, NARROW, NARROW, NARROW),
        in_specs=[SMEM] + [VMEM] * 8 + [ANY],
        out_specs=[VMEM] * 5,
        scratch_shapes=[
            pltpu.SMEM((NZ,), jnp.int32),
            pltpu.VMEM((TILES, BLOCK, COLS), BF16),
            pltpu.VMEM((NZ, DH, BLOCK), BF16),
            pltpu.VMEM((NZ, BLOCK, DH), BF16),
            pltpu.VMEM((NZ, BLOCK, 2 * DH), F32),
            pltpu.VMEM((DH, COLS), F32),
            pltpu.SemaphoreType.DMA((TILES,)),
        ],
        compiler_params=PARAMS,
        cost_estimate=cost(4, 0),
    )(turn, q, g, o, stat, *pieces, weights)


def ring(step):
    return [(i, (i + step) % NY) for i in range(NY)]


def exchange(x):
    return lax.all_to_all(x, Z, split_axis=0, concat_axis=0, tiled=True)


def spread(x):
    return exchange(x[0].reshape(ROWS, NZ, COLS).transpose(1, 0, 2))


def collect(x):
    return exchange(x).transpose(1, 0, 2).reshape(1, ROWS, H * DH)


def shards(queries, keys, values, grad_out, positions):
    kv = jnp.concatenate(
        [keys[0].reshape(ROWS, KVH, DH), values[0].reshape(ROWS, KVH, DH)], axis=2
    ).transpose(1, 0, 2)
    marks = jnp.concatenate([positions[0] // 64, positions[0] % 64]).astype(BF16)
    marks = jnp.broadcast_to(marks, (KVH, PADDED - ROWS, 2 * DH))
    kv = jnp.concatenate([kv, marks], axis=1)
    kv = exchange(jnp.repeat(kv, NZ // KVH, axis=0))
    own = positions[0, 0] // (2 * BLOCK)
    own = jnp.where(lax.axis_index("zhi") < NZ // 4, own, NZ // 2 - 1 - own)
    turn = jnp.bitwise_xor(own, lax.axis_index("outer")).astype(jnp.int32).reshape(1)
    pieces = (
        kv,
        lax.ppermute(kv, "y", ring(-1)),
        lax.ppermute(kv, "y", ring(2)),
        lax.ppermute(kv, "y", ring(1)),
    )
    q = spread(queries)
    out, stat, weights = run_forward(turn, q, pieces)
    g = spread(grad_out)
    dq, d0, d1, d2, d3 = run_backward(turn, q, g, out, stat, pieces, weights)
    out = collect(out)
    d1 = lax.ppermute(d1, "y", ring(1))
    d2 = lax.ppermute(d2, "y", ring(2))
    d3 = lax.ppermute(d3, "y", ring(-1))
    dq = collect(dq)
    wide = [d.astype(F32) for d in (d0, d1, d2, d3)]
    dkv = exchange(((wide[0] + wide[1]) + (wide[2] + wide[3])).astype(BF16))
    dkv = dkv.reshape(KVH, NZ // KVH, ROWS, 2 * DH).astype(F32).sum(axis=1)
    dkv = dkv.astype(BF16).transpose(1, 0, 2)
    dk = dkv[:, :, :DH].reshape(1, ROWS, KVH * DH)
    dv = dkv[:, :, DH:].reshape(1, ROWS, KVH * DH)
    return out, dq, dk, dv


def solution(mesh):
    devices = mesh.devices.reshape(NZ // 2, NY, mesh.shape["inner"], mesh.shape["outer"])
    fine = Mesh(devices, ("zhi", "y", "inner", "outer"))
    rows = P("inner", ("zhi", "y", "outer"), None)
    return jax.shard_map(
        shards,
        mesh=fine,
        in_specs=(rows, rows, rows, rows, P("inner", ("zhi", "y", "outer"))),
        out_specs=(rows, rows, rows, rows),
        check_vma=False,
    )
```

```python
import math

import jax
import jax.numpy as jnp
from jax import lax
from jax.experimental import pallas as pl
from jax.experimental.pallas import tpu as pltpu
from jax.sharding import Mesh, PartitionSpec as P

H = 32
KVH = 4
DH = 128
ROWS = 128
PADDED = 144
BLOCK = 512
NY = 4
NZ = 8
HEADS = H // NZ
COLS = HEADS * ROWS
TILES = NZ * (NZ + 1) // 2
NEGATIVE = -1e30
SCALE = 1.0 / math.sqrt(DH)
EXP2_SCALE = SCALE * math.log2(math.e)
Z = ("zhi", "outer")
DIMS_NT = (((1,), (1,)), ((), ()))
PLACES = (0, 2, 1, 3, 5, 7, 4, 6)
F32 = jnp.float32
BF16 = jnp.bfloat16


def flip(ref, z):
    return jnp.concatenate(
        [ref[z, :, i * DH : (i + 1) * DH].T for i in range(HEADS)], axis=1
    )


def unflip(ref, z, value):
    for i in range(HEADS):
        ref[z, :, i * DH : (i + 1) * DH] = value[:, i * ROWS : (i + 1) * ROWS].T


def fold(x, op):
    return op(x.reshape(x.shape[0] // 8, 8, x.shape[1]), axis=0)


def set_order(turn, order):
    for b in range(NZ):
        order[b] = jnp.bitwise_xor(turn[0], PLACES[b])


def tile_at(b, j):
    return b * (b + 1) // 2 + j


def forward(
    turn, q_ref, kv0, kv1, kv2, kv3, o_ref, stat_ref, p_hbm,
    order, s_buf, p_buf, k_n, v_t, out_acc, top_acc, sems,
):
    pieces = (kv0, kv1, kv2, kv3)
    set_order(turn, order)

    def row_marks(piece, z):
        row = piece[z, ROWS : ROWS + 16, :].astype(F32)[0:1]
        return row[:, :DH] * 64.0 + row[:, DH:]

    def enter(b):
        z = order[b]
        for rel in range(NY):
            cut = slice(rel * ROWS, (rel + 1) * ROWS)
            k_n[b, cut, :] = pieces[rel][z, :ROWS, :DH]
            v_t[b, :, cut] = pieces[rel][z, :ROWS, DH:].T
        q_t = flip(q_ref, z)
        s = jnp.dot(k_n[b], q_t, preferred_element_type=F32)
        q_marks = jnp.broadcast_to(row_marks(kv0, z), (ROWS, ROWS))
        slot = b % 2
        top = jnp.full((8, COLS), NEGATIVE, F32)
        for rel in range(NY):
            cut = slice(rel * ROWS, (rel + 1) * ROWS)
            k_marks = jnp.broadcast_to(row_marks(pieces[rel], z), (ROWS, ROWS)).T
            seen = k_marks <= q_marks
            part = jnp.concatenate(
                [
                    jnp.where(seen, s[cut, i * ROWS : (i + 1) * ROWS], NEGATIVE)
                    for i in range(HEADS)
                ],
                axis=1,
            )
            s_buf[slot, b, cut, :] = part
            top = jnp.maximum(top, fold(part, jnp.max))
        top_acc[...] = top
        return q_t

    def weigh(b, j, top):
        w = jnp.exp2((s_buf[b % 2, j] - top) * EXP2_SCALE)
        part = fold(w, jnp.sum)
        w = w.astype(BF16)
        tile = tile_at(b, j)
        p_buf[tile] = w
        out_acc[...] += jnp.dot(v_t[j], w, preferred_element_type=F32)
        return part

    def send(b, j):
        tile = tile_at(b, j)
        pltpu.make_async_copy(p_buf.at[tile], p_hbm.at[tile], sems.at[tile]).start()

    def leave(b, top, total):
        inv = 1.0 / jnp.sum(total, axis=0, keepdims=True)
        unflip(o_ref, order[b], (out_acc[...] * inv).astype(BF16))
        stat_ref[b] = inv

    enter(0)

    def group(b, carry):
        top = jnp.max(top_acc[...], axis=0, keepdims=True)
        q_next = enter(b + 1)
        out_acc[...] = jnp.zeros((DH, COLS), F32)

        def step(j, total):
            s = jnp.dot(k_n[j], q_next, preferred_element_type=F32)
            s_buf[(b + 1) % 2, j] = s
            top_acc[...] = jnp.maximum(top_acc[...], fold(s, jnp.max))
            total = total + weigh(b, j, top)
            send(b, j)
            return total

        total = lax.fori_loop(0, b + 1, step, jnp.zeros((8, COLS), F32))
        leave(b, top, total)
        return carry

    lax.fori_loop(0, NZ - 1, group, 0)
    last = NZ - 1
    top = jnp.max(top_acc[...], axis=0, keepdims=True)
    out_acc[...] = jnp.zeros((DH, COLS), F32)

    def step(j, total):
        total = total + weigh(last, j, top)
        send(last, j)
        return total

    total = lax.fori_loop(0, NZ, step, jnp.zeros((8, COLS), F32))
    leave(last, top, total)

    def wait(tile, carry):
        pltpu.make_async_copy(p_buf.at[tile], p_hbm.at[tile], sems.at[tile]).wait()
        return carry

    lax.fori_loop(0, TILES, wait, 0)


def backward(
    turn, q_ref, g_ref, o_ref, stat_ref, kv0, kv1, kv2, kv3, p_hbm,
    dq_ref, out0, out1, out2, out3,
    order, p_buf, k_t, v_n, acc, dq_acc, sems,
):
    pieces = (kv0, kv1, kv2, kv3)
    outs = (out0, out1, out2, out3)
    set_order(turn, order)

    def fetch(tile, carry):
        pltpu.make_async_copy(p_hbm.at[tile], p_buf.at[tile], sems.at[tile]).start()
        return carry

    lax.fori_loop(0, TILES, fetch, 0)

    def group(b, carry):
        z = order[b]
        for rel in range(NY):
            cut = slice(rel * ROWS, (rel + 1) * ROWS)
            k_t[b, :, cut] = pieces[rel][z, :ROWS, :DH].T
            v_n[b, cut, :] = pieces[rel][z, :ROWS, DH:]
        acc[b] = jnp.zeros((BLOCK, 2 * DH), F32)
        dq_acc[...] = jnp.zeros((DH, COLS), F32)
        q_t = flip(q_ref, z)
        g_t = flip(g_ref, z)
        o_t = flip(o_ref, z)
        inv = stat_ref[b]
        delta = jnp.sum(g_t.astype(F32) * o_t.astype(F32), axis=0, keepdims=True)
        q_n = (q_t.astype(F32) * inv).astype(BF16)
        g_n = (g_t.astype(F32) * inv).astype(BF16)

        def step(j, carry):
            tile = tile_at(b, j)
            pltpu.make_async_copy(p_hbm.at[tile], p_buf.at[tile], sems.at[tile]).wait()
            w = p_buf[tile]
            dp = jnp.dot(v_n[j], g_t, preferred_element_type=F32)
            ds = (w.astype(F32) * (dp - delta)).astype(BF16)
            acc[j, :, DH:] += lax.dot_general(w, g_n, DIMS_NT, preferred_element_type=F32)
            acc[j, :, :DH] += lax.dot_general(ds, q_n, DIMS_NT, preferred_element_type=F32)
            dq_acc[...] += jnp.dot(k_t[j], ds, preferred_element_type=F32)
            return carry

        lax.fori_loop(0, b + 1, step, 0)
        unflip(dq_ref, z, (dq_acc[...] * (inv * SCALE)).astype(BF16))
        return carry

    lax.fori_loop(0, NZ, group, 0)

    def finish(b, carry):
        z = order[b]
        for rel in range(NY):
            cut = slice(rel * ROWS, (rel + 1) * ROWS)
            outs[rel][z, :, :DH] = (acc[b, cut, :DH] * SCALE).astype(BF16)
            outs[rel][z, :, DH:] = acc[b, cut, DH:].astype(BF16)
        return carry

    lax.fori_loop(0, NZ, finish, 0)


VMEM = pl.BlockSpec(memory_space=pltpu.VMEM)
SMEM = pl.BlockSpec(memory_space=pltpu.SMEM)
ANY = pl.BlockSpec(memory_space=pl.ANY)
WIDE = jax.ShapeDtypeStruct((NZ, ROWS, COLS), BF16)
NARROW = jax.ShapeDtypeStruct((NZ, ROWS, 2 * DH), BF16)
WEIGHTS = jax.ShapeDtypeStruct((TILES, BLOCK, COLS), BF16)
STATS = jax.ShapeDtypeStruct((NZ, 1, COLS), F32)
PARAMS = pltpu.CompilerParams(vmem_limit_bytes=56 * 1024 * 1024)


def cost(matmuls, exps):
    return pl.CostEstimate(
        flops=TILES * matmuls * 2 * BLOCK * COLS * DH * 2,
        bytes_accessed=24 * 1024 * 1024,
        transcendentals=exps * TILES * BLOCK * COLS,
    )


def run_forward(turn, q, pieces):
    return pl.pallas_call(
        forward,
        name="forward",
        out_shape=(WIDE, STATS, WEIGHTS),
        in_specs=[SMEM] + [VMEM] * 5,
        out_specs=[VMEM, VMEM, ANY],
        scratch_shapes=[
            pltpu.SMEM((NZ,), jnp.int32),
            pltpu.VMEM((2, NZ, BLOCK, COLS), F32),
            pltpu.VMEM((TILES, BLOCK, COLS), BF16),
            pltpu.VMEM((NZ, BLOCK, DH), BF16),
            pltpu.VMEM((NZ, DH, BLOCK), BF16),
            pltpu.VMEM((DH, COLS), F32),
            pltpu.VMEM((8, COLS), F32),
            pltpu.SemaphoreType.DMA((TILES,)),
        ],
        compiler_params=PARAMS,
        cost_estimate=cost(2, 1),
    )(turn, q, *pieces)


def run_backward(turn, q, g, o, stat, pieces, weights):
    return pl.pallas_call(
        backward,
        name="backward",
        out_shape=(WIDE, NARROW, NARROW, NARROW, NARROW),
        in_specs=[SMEM] + [VMEM] * 8 + [ANY],
        out_specs=[VMEM] * 5,
        scratch_shapes=[
            pltpu.SMEM((NZ,), jnp.int32),
            pltpu.VMEM((TILES, BLOCK, COLS), BF16),
            pltpu.VMEM((NZ, DH, BLOCK), BF16),
            pltpu.VMEM((NZ, BLOCK, DH), BF16),
            pltpu.VMEM((NZ, BLOCK, 2 * DH), F32),
            pltpu.VMEM((DH, COLS), F32),
            pltpu.SemaphoreType.DMA((TILES,)),
        ],
        compiler_params=PARAMS,
        cost_estimate=cost(4, 0),
    )(turn, q, g, o, stat, *pieces, weights)


def ring(step):
    return [(i, (i + step) % NY) for i in range(NY)]


def exchange(x):
    return lax.all_to_all(x, Z, split_axis=0, concat_axis=0, tiled=True)


def after(x, *earlier):
    return lax.optimization_barrier((x, *earlier))[0]


def gather_y(kv):
    half = kv.shape[0] // 2
    up = lax.ppermute(kv, "y", ring(-1))
    down = lax.ppermute(kv, "y", ring(1))
    far = jnp.concatenate(
        [lax.ppermute(down[:half], "y", ring(1)), lax.ppermute(up[half:], "y", ring(-1))]
    )
    return kv, up, far, down


def add(x, y):
    return (x.astype(F32) + y.astype(F32)).astype(BF16)


def scatter_y(own, up, far, down):
    half = own.shape[0] // 2
    from_down = lax.ppermute(far[:half], "y", ring(1))
    from_up = lax.ppermute(far[half:], "y", ring(-1))
    up = jnp.concatenate([add(up[:half], from_down), up[half:]])
    down = jnp.concatenate([down[:half], add(down[half:], from_up)])
    up = lax.ppermute(up, "y", ring(1))
    down = lax.ppermute(down, "y", ring(-1))
    return (own.astype(F32) + (up.astype(F32) + down.astype(F32))).astype(BF16)


def chunks(x):
    return x[0].reshape(ROWS, NZ, COLS).transpose(1, 0, 2)


def shards(queries, keys, values, grad_out, positions):
    kv = jnp.concatenate(
        [keys[0].reshape(ROWS, KVH, DH), values[0].reshape(ROWS, KVH, DH)], axis=2
    ).transpose(1, 0, 2)
    marks = jnp.concatenate([positions[0] // 64, positions[0] % 64]).astype(BF16)
    marks = jnp.broadcast_to(marks, (KVH, PADDED - ROWS, 2 * DH))
    kv = jnp.concatenate([kv, marks], axis=1)
    kv = exchange(jnp.repeat(kv, NZ // KVH, axis=0))
    own = positions[0, 0] // (2 * BLOCK)
    own = jnp.where(lax.axis_index("zhi") < NZ // 4, own, NZ // 2 - 1 - own)
    turn = jnp.bitwise_xor(own, lax.axis_index("outer")).astype(jnp.int32).reshape(1)
    pieces = gather_y(kv)
    q = exchange(after(chunks(queries), kv))
    g = exchange(after(chunks(grad_out), q, *pieces))
    out, stat, weights = run_forward(turn, q, pieces)
    dq, d0, d1, d2, d3 = run_backward(turn, q, g, out, stat, pieces, weights)
    out = exchange(out)
    dq = exchange(after(dq, out))
    dkv = exchange(after(scatter_y(d0, d1, d2, d3), dq))
    dkv = dkv.reshape(KVH, NZ // KVH, ROWS, 2 * DH).astype(F32).sum(axis=1)
    dkv = dkv.astype(BF16).transpose(1, 0, 2)
    dk = dkv[:, :, :DH].reshape(1, ROWS, KVH * DH)
    dv = dkv[:, :, DH:].reshape(1, ROWS, KVH * DH)
    out = out.transpose(1, 0, 2).reshape(1, ROWS, H * DH)
    dq = dq.transpose(1, 0, 2).reshape(1, ROWS, H * DH)
    return out, dq, dk, dv


def solution(mesh):
    devices = mesh.devices.reshape(NZ // 2, NY, mesh.shape["inner"], mesh.shape["outer"])
    fine = Mesh(devices, ("zhi", "y", "inner", "outer"))
    rows = P("inner", ("zhi", "y", "outer"), None)
    return jax.shard_map(
        shards,
        mesh=fine,
        in_specs=(rows, rows, rows, rows, P("inner", ("zhi", "y", "outer"))),
        out_specs=(rows, rows, rows, rows),
        check_vma=False,
    )
```

```python
import math

import jax
import jax.numpy as jnp
from jax import lax
from jax.experimental import pallas as pl
from jax.experimental.pallas import tpu as pltpu
from jax.sharding import Mesh, PartitionSpec as P

H = 32
KVH = 4
DH = 128
ROWS = 128
PADDED = 144
BLOCK = 512
NY = 4
NH = 4
NZ = 2 * NH
PACK = H // NH
COLS = PACK * ROWS
TILES = NZ * (NZ + 1) // 4
NEGATIVE = -1e30
SCALE = 1.0 / math.sqrt(DH)
EXP2_SCALE = SCALE * math.log2(math.e)
DIMS_NT = (((1,), (1,)), ((), ()))
SLOTS = (0, 1, 4, 5, 6, 7, 2, 3)
F32 = jnp.float32
BF16 = jnp.bfloat16


def flip(ref, i):
    return jnp.concatenate([ref[i, :, k * DH : (k + 1) * DH].T for k in range(PACK)], axis=1)


def unflip(ref, i, value):
    for k in range(PACK):
        ref[i, :, k * DH : (k + 1) * DH] = value[:, k * ROWS : (k + 1) * ROWS].T


def fold(x, op):
    return op(x.reshape(x.shape[0] // 8, 8, x.shape[1]), axis=0)


def own_block(turn, n):
    return jnp.where(n < NH // 2, n + 2 * turn[0], n + NH - 2 * turn[0])


def turned(turn, slot):
    return (slot // NH) * NH + jnp.bitwise_and(slot - turn[1], NH - 1)


def key_slot(turn, slots, b):
    return turned(turn, jnp.bitwise_xor(slots[b], NH * turn[0]))


def set_slots(slots):
    for b in range(NZ):
        slots[b] = SLOTS[b]


def forward(
    turn, q_ref, kv0, kv1, kv2, kv3, o_ref, stat_ref, p_hbm,
    slots, s_buf, p_buf, k_n, v_t, out_acc, sems,
):
    pieces = (kv0, kv1, kv2, kv3)
    set_slots(slots)

    def row_marks(piece, z):
        row = piece[z, ROWS : ROWS + 16, :].astype(F32)[0:1]
        return row[:, :DH] * 64.0 + row[:, DH:]

    def prepare(b, carry):
        z = key_slot(turn, slots, b)
        for rel in range(NY):
            cut = slice(rel * ROWS, (rel + 1) * ROWS)
            k_n[b, cut, :] = pieces[rel][z, :ROWS, :DH]
            v_t[b, :, cut] = pieces[rel][z, :ROWS, DH:].T
        return carry

    lax.fori_loop(0, NZ, prepare, 0)

    def group(i, base):
        b = own_block(turn, i)
        z = turned(turn, i)
        q_t = flip(q_ref, i)
        out_acc[...] = jnp.zeros((DH, COLS), F32)

        def first(j, top):
            s = jnp.dot(k_n[j], q_t, preferred_element_type=F32)
            s_buf[j] = s
            return jnp.maximum(top, fold(s, jnp.max))

        top = lax.fori_loop(0, b, first, jnp.full((8, COLS), NEGATIVE, F32))
        s = jnp.dot(k_n[b], q_t, preferred_element_type=F32)
        q_marks = jnp.broadcast_to(row_marks(kv0, z), (ROWS, ROWS))
        for rel in range(NY):
            cut = slice(rel * ROWS, (rel + 1) * ROWS)
            k_marks = jnp.broadcast_to(row_marks(pieces[rel], z), (ROWS, ROWS)).T
            seen = k_marks <= q_marks
            part = jnp.concatenate(
                [
                    jnp.where(seen, s[cut, k * ROWS : (k + 1) * ROWS], NEGATIVE)
                    for k in range(PACK)
                ],
                axis=1,
            )
            s_buf[b, cut, :] = part
            top = jnp.maximum(top, fold(part, jnp.max))
        top = jnp.max(top, axis=0, keepdims=True)

        def second(j, total):
            w = jnp.exp2((s_buf[j] - top) * EXP2_SCALE)
            total = total + fold(w, jnp.sum)
            w = w.astype(BF16)
            tile = base + j
            p_buf[tile] = w
            out_acc[...] += jnp.dot(v_t[j], w, preferred_element_type=F32)
            pltpu.make_async_copy(p_buf.at[tile], p_hbm.at[tile], sems.at[tile]).start()
            return total

        total = lax.fori_loop(0, b + 1, second, jnp.zeros((8, COLS), F32))
        inv = 1.0 / jnp.sum(total, axis=0, keepdims=True)
        unflip(o_ref, i, (out_acc[...] * inv).astype(BF16))
        stat_ref[i] = inv
        return base + b + 1

    lax.fori_loop(0, NH, group, 0)

    def wait(tile, carry):
        pltpu.make_async_copy(p_buf.at[tile], p_hbm.at[tile], sems.at[tile]).wait()
        return carry

    lax.fori_loop(0, TILES, wait, 0)


def backward(
    turn, q_ref, g_ref, o_ref, stat_ref, kv0, kv1, kv2, kv3, p_hbm,
    dq_ref, out0, out1, out2, out3,
    slots, p_buf, k_t, v_n, acc, dq_acc, sems,
):
    pieces = (kv0, kv1, kv2, kv3)
    outs = (out0, out1, out2, out3)
    set_slots(slots)

    def fetch(tile, carry):
        pltpu.make_async_copy(p_hbm.at[tile], p_buf.at[tile], sems.at[tile]).start()
        return carry

    lax.fori_loop(0, TILES, fetch, 0)

    def prepare(b, carry):
        z = key_slot(turn, slots, b)
        for rel in range(NY):
            cut = slice(rel * ROWS, (rel + 1) * ROWS)
            k_t[b, :, cut] = pieces[rel][z, :ROWS, :DH].T
            v_n[b, cut, :] = pieces[rel][z, :ROWS, DH:]
        acc[b] = jnp.zeros((BLOCK, 2 * DH), F32)
        return carry

    lax.fori_loop(0, NZ, prepare, 0)

    def group(i, base):
        b = own_block(turn, i)
        dq_acc[...] = jnp.zeros((DH, COLS), F32)
        q_t = flip(q_ref, i)
        g_t = flip(g_ref, i)
        o_t = flip(o_ref, i)
        inv = stat_ref[i]
        delta = jnp.sum(g_t.astype(F32) * o_t.astype(F32), axis=0, keepdims=True)
        q_n = (q_t.astype(F32) * inv).astype(BF16)
        g_n = (g_t.astype(F32) * inv).astype(BF16)

        def step(j, carry):
            tile = base + j
            pltpu.make_async_copy(p_hbm.at[tile], p_buf.at[tile], sems.at[tile]).wait()
            w = p_buf[tile]
            dp = jnp.dot(v_n[j], g_t, preferred_element_type=F32)
            ds = (w.astype(F32) * (dp - delta)).astype(BF16)
            acc[j, :, DH:] += lax.dot_general(w, g_n, DIMS_NT, preferred_element_type=F32)
            acc[j, :, :DH] += lax.dot_general(ds, q_n, DIMS_NT, preferred_element_type=F32)
            dq_acc[...] += jnp.dot(k_t[j], ds, preferred_element_type=F32)
            return carry

        lax.fori_loop(0, b + 1, step, 0)
        unflip(dq_ref, i, (dq_acc[...] * (inv * SCALE)).astype(BF16))
        return base + b + 1

    lax.fori_loop(0, NH, group, 0)

    def finish(b, carry):
        slot = jnp.bitwise_xor(slots[b], NH * turn[0])
        z = (slot % NH) * 2 + jnp.bitwise_xor(slot // NH, turn[2])
        for rel in range(NY):
            cut = slice(rel * ROWS, (rel + 1) * ROWS)
            outs[rel][z, :, :DH] = (acc[b, cut, :DH] * SCALE).astype(BF16)
            outs[rel][z, :, DH:] = acc[b, cut, DH:].astype(BF16)
        return carry

    lax.fori_loop(0, NZ, finish, 0)


VMEM = pl.BlockSpec(memory_space=pltpu.VMEM)
SMEM = pl.BlockSpec(memory_space=pltpu.SMEM)
ANY = pl.BlockSpec(memory_space=pl.ANY)
WIDE = jax.ShapeDtypeStruct((NH, ROWS, COLS), BF16)
NARROW = jax.ShapeDtypeStruct((NZ, ROWS, 2 * DH), BF16)
WEIGHTS = jax.ShapeDtypeStruct((TILES, BLOCK, COLS), BF16)
STATS = jax.ShapeDtypeStruct((NH, 1, COLS), F32)
PARAMS = pltpu.CompilerParams(vmem_limit_bytes=56 * 1024 * 1024)


def cost(matmuls, exps):
    return pl.CostEstimate(
        flops=TILES * matmuls * 2 * BLOCK * COLS * DH * 2,
        bytes_accessed=24 * 1024 * 1024,
        transcendentals=exps * TILES * BLOCK * COLS,
    )


def run_forward(turn, q, pieces):
    return pl.pallas_call(
        forward,
        name="forward",
        out_shape=(WIDE, STATS, WEIGHTS),
        in_specs=[SMEM] + [VMEM] * 5,
        out_specs=[VMEM, VMEM, ANY],
        scratch_shapes=[
            pltpu.SMEM((NZ,), jnp.int32),
            pltpu.VMEM((NZ, BLOCK, COLS), F32),
            pltpu.VMEM((TILES, BLOCK, COLS), BF16),
            pltpu.VMEM((NZ, BLOCK, DH), BF16),
            pltpu.VMEM((NZ, DH, BLOCK), BF16),
            pltpu.VMEM((DH, COLS), F32),
            pltpu.SemaphoreType.DMA((TILES,)),
        ],
        compiler_params=PARAMS,
        cost_estimate=cost(2, 1),
    )(turn, q, *pieces)


def run_backward(turn, q, g, o, stat, pieces, weights):
    return pl.pallas_call(
        backward,
        name="backward",
        out_shape=(WIDE, NARROW, NARROW, NARROW, NARROW),
        in_specs=[SMEM] + [VMEM] * 8 + [ANY],
        out_specs=[VMEM] * 5,
        scratch_shapes=[
            pltpu.SMEM((NZ,), jnp.int32),
            pltpu.VMEM((TILES, BLOCK, COLS), BF16),
            pltpu.VMEM((NZ, DH, BLOCK), BF16),
            pltpu.VMEM((NZ, BLOCK, DH), BF16),
            pltpu.VMEM((NZ, BLOCK, 2 * DH), F32),
            pltpu.VMEM((DH, COLS), F32),
            pltpu.SemaphoreType.DMA((TILES,)),
        ],
        compiler_params=PARAMS,
        cost_estimate=cost(4, 0),
    )(turn, q, g, o, stat, *pieces, weights)


def ring(step):
    return [(i, (i + step) % NY) for i in range(NY)]


def hop(x, step):
    return lax.ppermute(x, "zhi", [(i, (i + step) % NH) for i in range(NH)])


def swap(x):
    return lax.ppermute(x, "outer", [(0, 1), (1, 0)])


def exchange(x):
    return lax.all_to_all(x, "zhi", split_axis=0, concat_axis=0, tiled=True)


def after(x, *earlier):
    return lax.optimization_barrier((x, *earlier))[0]


def gather_y(kv):
    half = kv.shape[0] // 2
    up = lax.ppermute(kv, "y", ring(-1))
    down = lax.ppermute(kv, "y", ring(1))
    far = jnp.concatenate(
        [lax.ppermute(down[:half], "y", ring(1)), lax.ppermute(up[half:], "y", ring(-1))]
    )
    return kv, up, far, down


def add(x, y):
    return (x.astype(F32) + y.astype(F32)).astype(BF16)


def scatter_y(own, up, far, down):
    half = own.shape[0] // 2
    from_down = lax.ppermute(far[:half], "y", ring(1))
    from_up = lax.ppermute(far[half:], "y", ring(-1))
    up = jnp.concatenate([add(up[:half], from_down), up[half:]])
    down = jnp.concatenate([down[:half], add(down[half:], from_up)])
    up = lax.ppermute(up, "y", ring(1))
    down = lax.ppermute(down, "y", ring(-1))
    return (own.astype(F32) + (up.astype(F32) + down.astype(F32))).astype(BF16)


def chunks(x):
    return x[0].reshape(ROWS, NH, COLS).transpose(1, 0, 2)


def rows(x):
    return x.transpose(1, 0, 2).reshape(1, ROWS, H * DH)


def shards(queries, keys, values, grad_out, positions):
    here = lax.axis_index("zhi").astype(jnp.int32)
    kv = jnp.concatenate(
        [keys[0].reshape(ROWS, KVH, DH), values[0].reshape(ROWS, KVH, DH)], axis=2
    ).transpose(1, 0, 2)
    marks = jnp.concatenate([positions[0] // 64, positions[0] % 64]).astype(BF16)
    marks = jnp.broadcast_to(marks, (KVH, PADDED - ROWS, 2 * DH))
    kv = jnp.concatenate([kv, marks], axis=1)
    own = positions[0, 0] // (2 * BLOCK)
    own = jnp.where(here < NH // 2, own, NH - 1 - own).astype(jnp.int32)
    parts = []
    for step in range(NH):
        part = lax.dynamic_index_in_dim(
            kv, jnp.bitwise_and(here - step, NH - 1), 0, keepdims=False
        )
        parts.append(hop(part, -step) if step else part)
    kv = jnp.stack(parts)
    turn = jnp.stack([own, here, lax.axis_index("outer").astype(jnp.int32)])
    kv = jnp.concatenate([kv, swap(kv)])
    pieces = gather_y(kv)
    q = exchange(after(chunks(queries), kv))
    g = exchange(after(chunks(grad_out), q, *pieces))
    out, stat, weights = run_forward(turn, q, pieces)
    dq, d0, d1, d2, d3 = run_backward(turn, q, g, out, stat, pieces, weights)
    out = exchange(out)
    dq = exchange(after(dq, out))
    dkv = after(scatter_y(d0, d1, d2, d3), dq)
    dkv = lax.all_to_all(dkv, ("zhi", "outer"), split_axis=0, concat_axis=0, tiled=True)
    dkv = dkv.reshape(NH, 2, ROWS, 2 * DH)
    dkv = add(dkv[:, 0], dkv[:, 1])
    dkv = dkv.transpose(1, 0, 2)
    dk = dkv[:, :, :DH].reshape(1, ROWS, KVH * DH)
    dv = dkv[:, :, DH:].reshape(1, ROWS, KVH * DH)
    return rows(out), rows(dq), dk, dv


def solution(mesh):
    devices = mesh.devices.reshape(NH, NY, mesh.shape["inner"], mesh.shape["outer"])
    fine = Mesh(devices, ("zhi", "y", "inner", "outer"))
    wide = P("inner", ("zhi", "y", "outer"), None)
    return jax.shard_map(
        shards,
        mesh=fine,
        in_specs=(wide, wide, wide, wide, P("inner", ("zhi", "y", "outer"))),
        out_specs=(wide, wide, wide, wide),
        check_vma=False,
    )
```

```python
import math

import jax
import jax.numpy as jnp
from jax import lax
from jax.experimental import pallas as pl
from jax.experimental.pallas import tpu as pltpu
from jax.sharding import Mesh, PartitionSpec as P

H = 32
KVH = 4
DH = 128
ROWS = 128
PADDED = 144
BLOCK = 512
NY = 4
NH = 4
NZ = 2 * NH
PACK = H // NH
COLS = PACK * ROWS
TILES = NZ * (NZ + 1) // 4
NEGATIVE = -1e30
SCALE = 1.0 / math.sqrt(DH)
EXP2_SCALE = SCALE * math.log2(math.e)
DIMS_NT = (((1,), (1,)), ((), ()))
SLOTS = (0, 1, 4, 5, 6, 7, 2, 3)
F32 = jnp.float32
BF16 = jnp.bfloat16


def flip(ref, i):
    return jnp.concatenate([ref[i, :, k * DH : (k + 1) * DH].T for k in range(PACK)], axis=1)


def unflip(ref, i, value):
    for k in range(PACK):
        ref[i, :, k * DH : (k + 1) * DH] = value[:, k * ROWS : (k + 1) * ROWS].T


def twice(count, step, carry):
    carry = lax.fori_loop(
        0, count // 2, lambda j, c: step(2 * j + 1, step(2 * j, c)), carry
    )
    return lax.fori_loop(count // 2 * 2, count, step, carry)


def fold(x, op):
    return op(x.reshape(x.shape[0] // 8, 8, x.shape[1]), axis=0)


def own_block(turn, n):
    return jnp.where(n < NH // 2, n + 2 * turn[0], n + NH - 2 * turn[0])


def turned(turn, slot):
    return (slot // NH) * NH + jnp.bitwise_and(slot - turn[1], NH - 1)


def key_slot(turn, slots, b):
    return turned(turn, jnp.bitwise_xor(slots[b], NH * turn[0]))


def set_slots(slots):
    for b in range(NZ):
        slots[b] = SLOTS[b]


def forward(
    turn, q_ref, kv0, kv1, kv2, kv3, o_ref, stat_ref, p_hbm,
    slots, s_buf, p_buf, k_n, v_t, out_acc, sems,
):
    pieces = (kv0, kv1, kv2, kv3)
    set_slots(slots)

    def row_marks(piece, z):
        row = piece[z, ROWS : ROWS + 16, :].astype(F32)[0:1]
        return row[:, :DH] * 64.0 + row[:, DH:]

    def prepare(b, carry):
        z = key_slot(turn, slots, b)
        for rel in range(NY):
            cut = slice(rel * ROWS, (rel + 1) * ROWS)
            k_n[b, cut, :] = pieces[rel][z, :ROWS, :DH]
            v_t[b, :, cut] = pieces[rel][z, :ROWS, DH:].T
        return carry

    lax.fori_loop(0, NZ, prepare, 0)

    def group(i, base):
        b = own_block(turn, i)
        z = turned(turn, i)
        q_t = flip(q_ref, i)
        out_acc[...] = jnp.zeros((DH, COLS), F32)

        def first(j, top):
            s = jnp.dot(k_n[j], q_t, preferred_element_type=F32)
            s_buf[j] = s
            return jnp.maximum(top, fold(s, jnp.max))

        top = twice(b, first, jnp.full((8, COLS), NEGATIVE, F32))
        s = jnp.dot(k_n[b], q_t, preferred_element_type=F32)
        q_marks = jnp.broadcast_to(row_marks(kv0, z), (ROWS, ROWS))
        for rel in range(NY):
            cut = slice(rel * ROWS, (rel + 1) * ROWS)
            k_marks = jnp.broadcast_to(row_marks(pieces[rel], z), (ROWS, ROWS)).T
            seen = k_marks <= q_marks
            part = jnp.concatenate(
                [
                    jnp.where(seen, s[cut, k * ROWS : (k + 1) * ROWS], NEGATIVE)
                    for k in range(PACK)
                ],
                axis=1,
            )
            s_buf[b, cut, :] = part
            top = jnp.maximum(top, fold(part, jnp.max))
        top = jnp.max(top, axis=0, keepdims=True)

        def second(j, total):
            w = jnp.exp2((s_buf[j] - top) * EXP2_SCALE)
            total = total + fold(w, jnp.sum)
            w = w.astype(BF16)
            tile = base + j
            p_buf[tile] = w
            out_acc[...] += jnp.dot(v_t[j], w, preferred_element_type=F32)
            pltpu.make_async_copy(p_buf.at[tile], p_hbm.at[tile], sems.at[tile]).start()
            return total

        total = twice(b + 1, second, jnp.zeros((8, COLS), F32))
        inv = 1.0 / jnp.sum(total, axis=0, keepdims=True)
        unflip(o_ref, i, (out_acc[...] * inv).astype(BF16))
        stat_ref[i] = inv
        return base + b + 1

    lax.fori_loop(0, NH, group, 0)

    def wait(tile, carry):
        pltpu.make_async_copy(p_buf.at[tile], p_hbm.at[tile], sems.at[tile]).wait()
        return carry

    lax.fori_loop(0, TILES, wait, 0)


def backward(
    turn, q_ref, g_ref, o_ref, stat_ref, kv0, kv1, kv2, kv3, p_hbm,
    dq_ref, low0, low1, low2, low3, high0, high1, high2, high3,
    slots, p_buf, k_t, v_n, acc, dq_acc, sems,
):
    pieces = (kv0, kv1, kv2, kv3)
    lows = (low0, low1, low2, low3)
    highs = (high0, high1, high2, high3)
    set_slots(slots)

    def fetch(tile, carry):
        pltpu.make_async_copy(p_hbm.at[tile], p_buf.at[tile], sems.at[tile]).start()
        return carry

    lax.fori_loop(0, TILES, fetch, 0)

    def prepare(b, carry):
        z = key_slot(turn, slots, b)
        for rel in range(NY):
            cut = slice(rel * ROWS, (rel + 1) * ROWS)
            k_t[b, :, cut] = pieces[rel][z, :ROWS, :DH].T
            v_n[b, cut, :] = pieces[rel][z, :ROWS, DH:]
        acc[b] = jnp.zeros((BLOCK, 2 * DH), F32)
        return carry

    lax.fori_loop(0, NZ, prepare, 0)

    def group(i, base):
        b = own_block(turn, i)
        dq_acc[...] = jnp.zeros((DH, COLS), F32)
        q_t = flip(q_ref, i)
        g_t = flip(g_ref, i)
        o_t = flip(o_ref, i)
        inv = stat_ref[i]
        delta = jnp.sum(g_t.astype(F32) * o_t.astype(F32), axis=0, keepdims=True)
        q_n = (q_t.astype(F32) * inv).astype(BF16)
        g_n = (g_t.astype(F32) * inv).astype(BF16)

        def step(j, carry):
            tile = base + j
            pltpu.make_async_copy(p_hbm.at[tile], p_buf.at[tile], sems.at[tile]).wait()
            w = p_buf[tile]
            dp = jnp.dot(v_n[j], g_t, preferred_element_type=F32)
            ds = (w.astype(F32) * (dp - delta)).astype(BF16)
            acc[j, :, DH:] += lax.dot_general(w, g_n, DIMS_NT, preferred_element_type=F32)
            acc[j, :, :DH] += lax.dot_general(ds, q_n, DIMS_NT, preferred_element_type=F32)
            dq_acc[...] += jnp.dot(k_t[j], ds, preferred_element_type=F32)
            return carry

        twice(b + 1, step, 0)
        unflip(dq_ref, i, (dq_acc[...] * (inv * SCALE)).astype(BF16))
        return base + b + 1

    lax.fori_loop(0, NH, group, 0)

    def finish(b, carry):
        slot = jnp.bitwise_xor(slots[b], NH * turn[0])
        z = (slot % NH) * 2 + jnp.bitwise_xor(slot // NH, turn[2])

        def store(outs, z):
            for rel in range(NY):
                cut = slice(rel * ROWS, (rel + 1) * ROWS)
                outs[rel][z, :, :DH] = (acc[b, cut, :DH] * SCALE).astype(BF16)
                outs[rel][z, :, DH:] = acc[b, cut, DH:].astype(BF16)

        pl.when(z < NH)(lambda: store(lows, z))
        pl.when(z >= NH)(lambda: store(highs, z - NH))
        return carry

    lax.fori_loop(0, NZ, finish, 0)


VMEM = pl.BlockSpec(memory_space=pltpu.VMEM)
SMEM = pl.BlockSpec(memory_space=pltpu.SMEM)
ANY = pl.BlockSpec(memory_space=pl.ANY)
WIDE = jax.ShapeDtypeStruct((NH, ROWS, COLS), BF16)
NARROW = jax.ShapeDtypeStruct((NH, ROWS, 2 * DH), BF16)
WEIGHTS = jax.ShapeDtypeStruct((TILES, BLOCK, COLS), BF16)
STATS = jax.ShapeDtypeStruct((NH, 1, COLS), F32)
PARAMS = pltpu.CompilerParams(vmem_limit_bytes=56 * 1024 * 1024)


def cost(matmuls, exps):
    return pl.CostEstimate(
        flops=TILES * matmuls * 2 * BLOCK * COLS * DH * 2,
        bytes_accessed=24 * 1024 * 1024,
        transcendentals=exps * TILES * BLOCK * COLS,
    )


def run_forward(turn, q, pieces):
    return pl.pallas_call(
        forward,
        name="forward",
        out_shape=(WIDE, STATS, WEIGHTS),
        in_specs=[SMEM] + [VMEM] * 5,
        out_specs=[VMEM, VMEM, ANY],
        scratch_shapes=[
            pltpu.SMEM((NZ,), jnp.int32),
            pltpu.VMEM((NZ, BLOCK, COLS), F32),
            pltpu.VMEM((TILES, BLOCK, COLS), BF16),
            pltpu.VMEM((NZ, BLOCK, DH), BF16),
            pltpu.VMEM((NZ, DH, BLOCK), BF16),
            pltpu.VMEM((DH, COLS), F32),
            pltpu.SemaphoreType.DMA((TILES,)),
        ],
        compiler_params=PARAMS,
        cost_estimate=cost(2, 1),
    )(turn, q, *pieces)


def run_backward(turn, q, g, o, stat, pieces, weights):
    return pl.pallas_call(
        backward,
        name="backward",
        out_shape=(WIDE,) + (NARROW,) * (2 * NY),
        in_specs=[SMEM] + [VMEM] * 8 + [ANY],
        out_specs=[VMEM] * (1 + 2 * NY),
        scratch_shapes=[
            pltpu.SMEM((NZ,), jnp.int32),
            pltpu.VMEM((TILES, BLOCK, COLS), BF16),
            pltpu.VMEM((NZ, DH, BLOCK), BF16),
            pltpu.VMEM((NZ, BLOCK, DH), BF16),
            pltpu.VMEM((NZ, BLOCK, 2 * DH), F32),
            pltpu.VMEM((DH, COLS), F32),
            pltpu.SemaphoreType.DMA((TILES,)),
        ],
        compiler_params=PARAMS,
        cost_estimate=cost(4, 0),
    )(turn, q, g, o, stat, *pieces, weights)


def ring(step):
    return [(i, (i + step) % NY) for i in range(NY)]


def hop(x, step):
    return lax.ppermute(x, "zhi", [(i, (i + step) % NH) for i in range(NH)])


def swap(x):
    return lax.ppermute(x, "outer", [(0, 1), (1, 0)])


def exchange(x):
    return lax.all_to_all(x, "zhi", split_axis=0, concat_axis=0, tiled=True)


def after(x, *earlier):
    return lax.optimization_barrier((x, *earlier))[0]


def gather_y(kv):
    half = kv.shape[0] // 2
    up = lax.ppermute(kv, "y", ring(-1))
    down = lax.ppermute(kv, "y", ring(1))
    far = jnp.concatenate(
        [lax.ppermute(down[:half], "y", ring(1)), lax.ppermute(up[half:], "y", ring(-1))]
    )
    return kv, up, far, down


def add(x, y):
    return (x.astype(F32) + y.astype(F32)).astype(BF16)


def scatter_y(own, up, far, down):
    from_down = lax.ppermute(far[0], "y", ring(1))
    from_up = lax.ppermute(far[1], "y", ring(-1))
    up = (lax.ppermute(add(up[0], from_down), "y", ring(1)), lax.ppermute(up[1], "y", ring(1)))
    down = (
        lax.ppermute(down[0], "y", ring(-1)),
        lax.ppermute(add(down[1], from_up), "y", ring(-1)),
    )
    return jnp.concatenate(
        [
            (o.astype(F32) + (u.astype(F32) + d.astype(F32))).astype(BF16)
            for o, u, d in zip(own, up, down)
        ]
    )


def chunks(x):
    return x[0].reshape(ROWS, NH, COLS).transpose(1, 0, 2)


def rows(x):
    return x.transpose(1, 0, 2).reshape(1, ROWS, H * DH)


def shards(queries, keys, values, grad_out, positions):
    here = lax.axis_index("zhi").astype(jnp.int32)
    kv = jnp.concatenate(
        [keys[0].reshape(ROWS, KVH, DH), values[0].reshape(ROWS, KVH, DH)], axis=2
    ).transpose(1, 0, 2)
    marks = jnp.concatenate([positions[0] // 64, positions[0] % 64]).astype(BF16)
    marks = jnp.broadcast_to(marks, (KVH, PADDED - ROWS, 2 * DH))
    kv = jnp.concatenate([kv, marks], axis=1)
    own = positions[0, 0] // (2 * BLOCK)
    own = jnp.where(here < NH // 2, own, NH - 1 - own).astype(jnp.int32)
    parts = []
    for step in range(NH):
        part = lax.dynamic_index_in_dim(
            kv, jnp.bitwise_and(here - step, NH - 1), 0, keepdims=False
        )
        parts.append(hop(part, -step) if step else part)
    kv = jnp.stack(parts)
    turn = jnp.stack([own, here, lax.axis_index("outer").astype(jnp.int32)])
    kv = jnp.concatenate([kv, swap(kv)])
    pieces = gather_y(kv)
    q = exchange(after(chunks(queries), kv))
    g = exchange(after(chunks(grad_out), q, *pieces))
    out, stat, weights = run_forward(turn, q, pieces)
    dq, *halves = run_backward(turn, q, g, out, stat, pieces, weights)
    out = exchange(out)
    dq = exchange(after(dq, out))
    dkv = after(scatter_y(*zip(halves[:NY], halves[NY:])), dq)
    dkv = lax.all_to_all(dkv, ("zhi", "outer"), split_axis=0, concat_axis=0, tiled=True)
    dkv = dkv.reshape(NH, 2, ROWS, 2 * DH)
    dkv = add(dkv[:, 0], dkv[:, 1])
    dkv = dkv.transpose(1, 0, 2)
    dk = dkv[:, :, :DH].reshape(1, ROWS, KVH * DH)
    dv = dkv[:, :, DH:].reshape(1, ROWS, KVH * DH)
    return rows(out), rows(dq), dk, dv


def solution(mesh):
    devices = mesh.devices.reshape(NH, NY, mesh.shape["inner"], mesh.shape["outer"])
    fine = Mesh(devices, ("zhi", "y", "inner", "outer"))
    wide = P("inner", ("zhi", "y", "outer"), None)
    return jax.shard_map(
        shards,
        mesh=fine,
        in_specs=(wide, wide, wide, wide, P("inner", ("zhi", "y", "outer"))),
        out_specs=(wide, wide, wide, wide),
        check_vma=False,
    )
```

```python
import math

import jax
import jax.numpy as jnp
from jax import lax
from jax.experimental import pallas as pl
from jax.experimental.pallas import tpu as pltpu
from jax.sharding import Mesh, PartitionSpec as P

H = 32
KVH = 4
DH = 128
ROWS = 128
PADDED = 144
BLOCK = 512
NY = 4
NH = 4
NZ = 2 * NH
PACK = H // NH
COLS = PACK * ROWS
TILES = NZ * (NZ + 1) // 4
NEGATIVE = -1e30
SCALE = 1.0 / math.sqrt(DH)
EXP2_SCALE = SCALE * math.log2(math.e)
DIMS_NT = (((1,), (1,)), ((), ()))
SLOTS = (0, 1, 4, 5, 6, 7, 2, 3)
F32 = jnp.float32
BF16 = jnp.bfloat16


def flip(ref, i):
    return jnp.concatenate([ref[i, :, k * DH : (k + 1) * DH].T for k in range(PACK)], axis=1)


def unflip(ref, i, value):
    for k in range(PACK):
        ref[i, :, k * DH : (k + 1) * DH] = value[:, k * ROWS : (k + 1) * ROWS].T


def twice(count, step, carry):
    carry = lax.fori_loop(
        0, count // 2, lambda j, c: step(2 * j + 1, step(2 * j, c)), carry
    )
    return lax.fori_loop(count // 2 * 2, count, step, carry)


def fold(x, op):
    return op(x.reshape(x.shape[0] // 8, 8, x.shape[1]), axis=0)


def own_block(turn, n):
    return jnp.where(n < NH // 2, n + 2 * turn[0], n + NH - 2 * turn[0])


def turned(turn, slot):
    return (slot // NH) * NH + jnp.bitwise_and(slot - turn[1], NH - 1)


def key_slot(turn, slots, b):
    return turned(turn, jnp.bitwise_xor(slots[b], NH * turn[0]))


def set_slots(slots):
    for b in range(NZ):
        slots[b] = SLOTS[b]


def forward(
    turn, q_ref, kv0, kv1, kv2, kv3, o_ref, stat_ref, p_hbm,
    slots, s_buf, p_buf, k_n, v_t, out_acc, sems,
):
    pieces = (kv0, kv1, kv2, kv3)
    set_slots(slots)

    def row_marks(piece, z):
        row = piece[z, ROWS : ROWS + 16, :].astype(F32)[0:1]
        return row[:, :DH] * 64.0 + row[:, DH:]

    def prepare(b, carry):
        z = key_slot(turn, slots, b)
        for rel in range(NY):
            cut = slice(rel * ROWS, (rel + 1) * ROWS)
            k_n[b, cut, :] = pieces[rel][z, :ROWS, :DH]
            v_t[b, :, cut] = pieces[rel][z, :ROWS, DH:].T
        return carry

    lax.fori_loop(0, NZ, prepare, 0)

    def group(i, base):
        b = own_block(turn, i)
        z = turned(turn, i)
        q_t = flip(q_ref, i)
        out_acc[...] = jnp.zeros((DH, COLS), F32)

        def first(j, top):
            s = jnp.dot(k_n[j], q_t, preferred_element_type=F32)
            s_buf[j] = s
            return jnp.maximum(top, fold(s, jnp.max))

        top = twice(b, first, jnp.full((8, COLS), NEGATIVE, F32))
        s = jnp.dot(k_n[b], q_t, preferred_element_type=F32)
        q_marks = jnp.broadcast_to(row_marks(kv0, z), (ROWS, ROWS))
        for rel in range(NY):
            cut = slice(rel * ROWS, (rel + 1) * ROWS)
            k_marks = jnp.broadcast_to(row_marks(pieces[rel], z), (ROWS, ROWS)).T
            seen = k_marks <= q_marks
            part = jnp.concatenate(
                [
                    jnp.where(seen, s[cut, k * ROWS : (k + 1) * ROWS], NEGATIVE)
                    for k in range(PACK)
                ],
                axis=1,
            )
            s_buf[b, cut, :] = part
            top = jnp.maximum(top, fold(part, jnp.max))
        top = jnp.max(top, axis=0, keepdims=True)

        def second(j, total):
            w = jnp.exp2((s_buf[j] - top) * EXP2_SCALE)
            total = total + fold(w, jnp.sum)
            w = w.astype(BF16)
            tile = base + j
            p_buf[tile] = w
            out_acc[...] += jnp.dot(v_t[j], w, preferred_element_type=F32)
            pltpu.make_async_copy(p_buf.at[tile], p_hbm.at[tile], sems.at[tile]).start()
            return total

        total = twice(b + 1, second, jnp.zeros((8, COLS), F32))
        inv = 1.0 / jnp.sum(total, axis=0, keepdims=True)
        unflip(o_ref, i, (out_acc[...] * inv).astype(BF16))
        stat_ref[i] = inv
        return base + b + 1

    lax.fori_loop(0, NH, group, 0)

    def wait(tile, carry):
        pltpu.make_async_copy(p_buf.at[tile], p_hbm.at[tile], sems.at[tile]).wait()
        return carry

    lax.fori_loop(0, TILES, wait, 0)


def backward(
    turn, q_ref, g_ref, o_ref, stat_ref, kv0, kv1, kv2, kv3, p_hbm,
    dq_ref, low0, low1, low2, low3, high0, high1, high2, high3,
    slots, p_buf, k_t, v_n, acc, dq_acc, sems,
):
    pieces = (kv0, kv1, kv2, kv3)
    lows = (low0, low1, low2, low3)
    highs = (high0, high1, high2, high3)
    set_slots(slots)

    def fetch(tile, carry):
        pltpu.make_async_copy(p_hbm.at[tile], p_buf.at[tile], sems.at[tile]).start()
        return carry

    lax.fori_loop(0, TILES, fetch, 0)

    def prepare(b, carry):
        z = key_slot(turn, slots, b)
        for rel in range(NY):
            cut = slice(rel * ROWS, (rel + 1) * ROWS)
            k_t[b, :, cut] = pieces[rel][z, :ROWS, :DH].T
            v_n[b, cut, :] = pieces[rel][z, :ROWS, DH:]
        acc[b] = jnp.zeros((BLOCK, 2 * DH), F32)
        return carry

    lax.fori_loop(0, NZ, prepare, 0)

    def group(i, base):
        b = own_block(turn, i)
        dq_acc[...] = jnp.zeros((DH, COLS), F32)
        q_t = flip(q_ref, i)
        g_t = flip(g_ref, i)
        o_t = flip(o_ref, i)
        inv = stat_ref[i]
        delta = jnp.sum(g_t.astype(F32) * o_t.astype(F32), axis=0, keepdims=True)
        q_n = (q_t.astype(F32) * inv).astype(BF16)
        g_n = (g_t.astype(F32) * inv).astype(BF16)

        def step(j, carry):
            tile = base + j
            pltpu.make_async_copy(p_hbm.at[tile], p_buf.at[tile], sems.at[tile]).wait()
            w = p_buf[tile]
            dp = jnp.dot(v_n[j], g_t, preferred_element_type=F32)
            ds = (w.astype(F32) * (dp - delta)).astype(BF16)
            acc[j, :, DH:] += lax.dot_general(w, g_n, DIMS_NT, preferred_element_type=F32)
            acc[j, :, :DH] += lax.dot_general(ds, q_n, DIMS_NT, preferred_element_type=F32)
            dq_acc[...] += jnp.dot(k_t[j], ds, preferred_element_type=F32)
            return carry

        twice(b + 1, step, 0)
        unflip(dq_ref, i, (dq_acc[...] * (inv * SCALE)).astype(BF16))
        return base + b + 1

    lax.fori_loop(0, NH, group, 0)

    def finish(b, carry):
        slot = jnp.bitwise_xor(slots[b], NH * turn[0])
        z = (slot % NH) * 2 + jnp.bitwise_xor(slot // NH, turn[2])

        def store(outs, z):
            for rel in range(NY):
                cut = slice(rel * ROWS, (rel + 1) * ROWS)
                outs[rel][z, :, :DH] = (acc[b, cut, :DH] * SCALE).astype(BF16)
                outs[rel][z, :, DH:] = acc[b, cut, DH:].astype(BF16)

        pl.when(z < NH)(lambda: store(lows, z))
        pl.when(z >= NH)(lambda: store(highs, z - NH))
        return carry

    lax.fori_loop(0, NZ, finish, 0)


VMEM = pl.BlockSpec(memory_space=pltpu.VMEM)
SMEM = pl.BlockSpec(memory_space=pltpu.SMEM)
ANY = pl.BlockSpec(memory_space=pl.ANY)
WIDE = jax.ShapeDtypeStruct((NH, ROWS, COLS), BF16)
NARROW = jax.ShapeDtypeStruct((NH, ROWS, 2 * DH), BF16)
WEIGHTS = jax.ShapeDtypeStruct((TILES, BLOCK, COLS), BF16)
STATS = jax.ShapeDtypeStruct((NH, 1, COLS), F32)
PARAMS = pltpu.CompilerParams(vmem_limit_bytes=56 * 1024 * 1024)


def cost(matmuls, exps):
    return pl.CostEstimate(
        flops=TILES * matmuls * 2 * BLOCK * COLS * DH * 2,
        bytes_accessed=24 * 1024 * 1024,
        transcendentals=exps * TILES * BLOCK * COLS,
    )


def run_forward(turn, q, pieces):
    return pl.pallas_call(
        forward,
        name="forward",
        out_shape=(WIDE, STATS, WEIGHTS),
        in_specs=[SMEM] + [VMEM] * 5,
        out_specs=[VMEM, VMEM, ANY],
        scratch_shapes=[
            pltpu.SMEM((NZ,), jnp.int32),
            pltpu.VMEM((NZ, BLOCK, COLS), F32),
            pltpu.VMEM((TILES, BLOCK, COLS), BF16),
            pltpu.VMEM((NZ, BLOCK, DH), BF16),
            pltpu.VMEM((NZ, DH, BLOCK), BF16),
            pltpu.VMEM((DH, COLS), F32),
            pltpu.SemaphoreType.DMA((TILES,)),
        ],
        compiler_params=PARAMS,
        cost_estimate=cost(2, 1),
    )(turn, q, *pieces)


def run_backward(turn, q, g, o, stat, pieces, weights):
    return pl.pallas_call(
        backward,
        name="backward",
        out_shape=(WIDE,) + (NARROW,) * (2 * NY),
        in_specs=[SMEM] + [VMEM] * 8 + [ANY],
        out_specs=[VMEM] * (1 + 2 * NY),
        scratch_shapes=[
            pltpu.SMEM((NZ,), jnp.int32),
            pltpu.VMEM((TILES, BLOCK, COLS), BF16),
            pltpu.VMEM((NZ, DH, BLOCK), BF16),
            pltpu.VMEM((NZ, BLOCK, DH), BF16),
            pltpu.VMEM((NZ, BLOCK, 2 * DH), F32),
            pltpu.VMEM((DH, COLS), F32),
            pltpu.SemaphoreType.DMA((TILES,)),
        ],
        compiler_params=PARAMS,
        cost_estimate=cost(4, 0),
    )(turn, q, g, o, stat, *pieces, weights)


def ring(step):
    return [(i, (i + step) % NY) for i in range(NY)]


def hop(x, step):
    return lax.ppermute(x, "zhi", [(i, (i + step) % NH) for i in range(NH)])


def swap(x):
    return lax.ppermute(x, "outer", [(0, 1), (1, 0)])


def exchange(x):
    return lax.all_to_all(x, "zhi", split_axis=0, concat_axis=0, tiled=True)


def after(x, *earlier):
    return lax.optimization_barrier((x, *earlier))[0]


def gather_y(kv):
    half = kv.shape[0] // 2
    up = lax.ppermute(kv, "y", ring(-1))
    down = lax.ppermute(kv, "y", ring(1))
    far = jnp.concatenate(
        [lax.ppermute(down[:half], "y", ring(1)), lax.ppermute(up[half:], "y", ring(-1))]
    )
    return kv, up, far, down


def add(x, y):
    return (x.astype(F32) + y.astype(F32)).astype(BF16)


def scatter_y(own, up, far, down):
    from_down = lax.ppermute(far[0], "y", ring(1))
    from_up = lax.ppermute(far[1], "y", ring(-1))
    up = (lax.ppermute(add(up[0], from_down), "y", ring(1)), lax.ppermute(up[1], "y", ring(1)))
    down = (
        lax.ppermute(down[0], "y", ring(-1)),
        lax.ppermute(add(down[1], from_up), "y", ring(-1)),
    )
    return jnp.concatenate(
        [
            (o.astype(F32) + (u.astype(F32) + d.astype(F32))).astype(BF16)
            for o, u, d in zip(own, up, down)
        ]
    )


def chunks(x):
    return x[0].reshape(ROWS, NH, COLS).transpose(1, 0, 2)


def rows(x):
    return x.transpose(1, 0, 2).reshape(1, ROWS, H * DH)


def shards(queries, keys, values, grad_out, positions):
    here = lax.axis_index("zhi").astype(jnp.int32)
    marks = jnp.concatenate([positions[0] // 64, positions[0] % 64]).astype(BF16)
    marks = jnp.broadcast_to(marks, (PADDED - ROWS, 2 * DH))
    own = lax.shift_right_logical(positions[0, 0], int(math.log2(2 * BLOCK)))
    own = jnp.where(here < NH // 2, own, NH - 1 - own).astype(jnp.int32)
    parts = []
    for step in range(NH):
        start = jnp.bitwise_and(here - step, NH - 1) * DH
        heads = [lax.dynamic_slice(x[0], (0, start), (ROWS, DH)) for x in (keys, values)]
        part = jnp.concatenate([jnp.concatenate(heads, axis=1), marks])
        parts.append(hop(part, -step) if step else part)
    kv = jnp.stack(parts)
    turn = jnp.stack([own, here, lax.axis_index("outer").astype(jnp.int32)])
    kv = jnp.concatenate([kv, swap(kv)])
    pieces = gather_y(kv)
    q, turn, _ = lax.optimization_barrier((chunks(queries), turn, kv))
    q = exchange(q)
    g = exchange(after(chunks(grad_out), q, *pieces))
    out, stat, weights = run_forward(turn, q, pieces)
    dq, *halves = run_backward(turn, q, g, out, stat, pieces, weights)
    out = exchange(out)
    dq = exchange(after(dq, out))
    dkv = after(scatter_y(*zip(halves[:NY], halves[NY:])), dq)
    dkv = lax.all_to_all(dkv, ("zhi", "outer"), split_axis=0, concat_axis=0, tiled=True)
    dkv = dkv.reshape(NH, 2, ROWS, 2 * DH)
    dkv = add(dkv[:, 0], dkv[:, 1])
    dk = jnp.concatenate([dkv[n, :, :DH] for n in range(KVH)], axis=1)[None]
    dv = jnp.concatenate([dkv[n, :, DH:] for n in range(KVH)], axis=1)[None]
    return rows(out), rows(dq), dk, dv


def solution(mesh):
    devices = mesh.devices.reshape(NH, NY, mesh.shape["inner"], mesh.shape["outer"])
    fine = Mesh(devices, ("zhi", "y", "inner", "outer"))
    wide = P("inner", ("zhi", "y", "outer"), None)
    return jax.shard_map(
        shards,
        mesh=fine,
        in_specs=(wide, wide, wide, wide, P("inner", ("zhi", "y", "outer"))),
        out_specs=(wide, wide, wide, wide),
        check_vma=False,
    )
```

```python
import math

import jax
import jax.numpy as jnp
from jax import lax
from jax.experimental import pallas as pl
from jax.experimental.pallas import tpu as pltpu
from jax.sharding import Mesh, PartitionSpec as P

H = 32
KVH = 4
DH = 128
ROWS = 128
PADDED = 144
BLOCK = 512
NY = 4
NH = 4
NZ = 2 * NH
PACK = H // NH
COLS = PACK * ROWS
TILES = NZ * (NZ + 1) // 4
NEGATIVE = -1e30
SCALE = 1.0 / math.sqrt(DH)
EXP2_SCALE = SCALE * math.log2(math.e)
DIMS_NT = (((1,), (1,)), ((), ()))
SLOTS = (0, 1, 4, 5, 6, 7, 2, 3)
F32 = jnp.float32
BF16 = jnp.bfloat16


def flip(ref, i):
    return jnp.concatenate([ref[i, :, k * DH : (k + 1) * DH].T for k in range(PACK)], axis=1)


def unflip(ref, i, value):
    for k in range(PACK):
        ref[i, :, k * DH : (k + 1) * DH] = value[:, k * ROWS : (k + 1) * ROWS].T


def twice(count, step, carry):
    carry = lax.fori_loop(
        0, count // 2, lambda j, c: step(2 * j + 1, step(2 * j, c)), carry
    )
    return lax.fori_loop(count // 2 * 2, count, step, carry)


def fold(x, op):
    return op(x.reshape(x.shape[0] // 8, 8, x.shape[1]), axis=0)


def own_block(turn, n):
    return jnp.where(n < NH // 2, n + 2 * turn[0], n + NH - 2 * turn[0])


def turned(turn, slot):
    return (slot // NH) * NH + jnp.bitwise_and(slot - turn[1], NH - 1)


def key_slot(turn, slots, b):
    return turned(turn, jnp.bitwise_xor(slots[b], NH * turn[0]))


def set_slots(slots):
    for b in range(NZ):
        slots[b] = SLOTS[b]


def forward(
    turn, q_ref, kv0, kv1, kv2, kv3, o_ref, stat_ref, p_hbm,
    slots, s_buf, p_buf, k_n, v_t, out_acc, sems,
):
    pieces = (kv0, kv1, kv2, kv3)
    set_slots(slots)

    def row_marks(piece, z):
        row = piece[z, ROWS : ROWS + 16, :].astype(F32)[0:1]
        return row[:, :DH] * 64.0 + row[:, DH:]

    def prepare(b, carry):
        z = key_slot(turn, slots, b)
        for rel in range(NY):
            cut = slice(rel * ROWS, (rel + 1) * ROWS)
            k_n[b, cut, :] = pieces[rel][z, :ROWS, :DH]
            v_t[b, :, cut] = pieces[rel][z, :ROWS, DH:].T
        return carry

    lax.fori_loop(0, NZ, prepare, 0)

    def group(i, base):
        b = own_block(turn, i)
        z = turned(turn, i)
        q_t = flip(q_ref, i)
        out_acc[...] = jnp.zeros((DH, COLS), F32)

        def first(j, top):
            s = jnp.dot(k_n[j], q_t, preferred_element_type=F32)
            s_buf[j] = s
            return jnp.maximum(top, fold(s, jnp.max))

        top = twice(b, first, jnp.full((8, COLS), NEGATIVE, F32))
        s = jnp.dot(k_n[b], q_t, preferred_element_type=F32)
        q_marks = jnp.broadcast_to(row_marks(kv0, z), (ROWS, ROWS))
        for rel in range(NY):
            cut = slice(rel * ROWS, (rel + 1) * ROWS)
            k_marks = jnp.broadcast_to(row_marks(pieces[rel], z), (ROWS, ROWS)).T
            seen = k_marks <= q_marks
            part = jnp.concatenate(
                [
                    jnp.where(seen, s[cut, k * ROWS : (k + 1) * ROWS], NEGATIVE)
                    for k in range(PACK)
                ],
                axis=1,
            )
            s_buf[b, cut, :] = part
            top = jnp.maximum(top, fold(part, jnp.max))
        top = jnp.max(top, axis=0, keepdims=True)

        def second(j, total):
            w = jnp.exp2((s_buf[j] - top) * EXP2_SCALE)
            total = total + fold(w, jnp.sum)
            w = w.astype(BF16)
            tile = base + j
            p_buf[tile] = w
            out_acc[...] += jnp.dot(v_t[j], w, preferred_element_type=F32)
            pltpu.make_async_copy(p_buf.at[tile], p_hbm.at[tile], sems.at[tile]).start()
            return total

        total = twice(b + 1, second, jnp.zeros((8, COLS), F32))
        inv = 1.0 / jnp.sum(total, axis=0, keepdims=True)
        unflip(o_ref, i, (out_acc[...] * inv).astype(BF16))
        stat_ref[i] = inv
        return base + b + 1

    lax.fori_loop(0, NH, group, 0)

    def wait(tile, carry):
        pltpu.make_async_copy(p_buf.at[tile], p_hbm.at[tile], sems.at[tile]).wait()
        return carry

    lax.fori_loop(0, TILES, wait, 0)


def backward(
    turn, q_ref, g_ref, o_ref, stat_ref, kv0, kv1, kv2, kv3, p_hbm,
    dq_ref, low0, low1, low2, low3, high0, high1, high2, high3,
    slots, p_buf, k_t, v_n, acc, dq_acc, sems,
):
    pieces = (kv0, kv1, kv2, kv3)
    lows = (low0, low1, low2, low3)
    highs = (high0, high1, high2, high3)
    set_slots(slots)

    def fetch(tile, carry):
        pltpu.make_async_copy(p_hbm.at[tile], p_buf.at[tile], sems.at[tile]).start()
        return carry

    lax.fori_loop(0, TILES, fetch, 0)

    def prepare(b, carry):
        z = key_slot(turn, slots, b)
        for rel in range(NY):
            cut = slice(rel * ROWS, (rel + 1) * ROWS)
            k_t[b, :, cut] = pieces[rel][z, :ROWS, :DH].T
            v_n[b, cut, :] = pieces[rel][z, :ROWS, DH:]
        acc[b] = jnp.zeros((BLOCK, 2 * DH), F32)
        return carry

    lax.fori_loop(0, NZ, prepare, 0)

    def group(i, base):
        b = own_block(turn, i)
        dq_acc[...] = jnp.zeros((DH, COLS), F32)
        q_t = flip(q_ref, i)
        g_t = flip(g_ref, i)
        o_t = flip(o_ref, i)
        inv = stat_ref[i]
        delta = jnp.sum(g_t.astype(F32) * o_t.astype(F32), axis=0, keepdims=True)
        q_n = (q_t.astype(F32) * inv).astype(BF16)
        g_n = (g_t.astype(F32) * inv).astype(BF16)

        def step(j, carry):
            tile = base + j
            pltpu.make_async_copy(p_hbm.at[tile], p_buf.at[tile], sems.at[tile]).wait()
            w = p_buf[tile]
            dp = jnp.dot(v_n[j], g_t, preferred_element_type=F32)
            ds = (w.astype(F32) * (dp - delta)).astype(BF16)
            acc[j, :, DH:] += lax.dot_general(w, g_n, DIMS_NT, preferred_element_type=F32)
            acc[j, :, :DH] += lax.dot_general(ds, q_n, DIMS_NT, preferred_element_type=F32)
            dq_acc[...] += jnp.dot(k_t[j], ds, preferred_element_type=F32)
            return carry

        twice(b + 1, step, 0)
        unflip(dq_ref, i, (dq_acc[...] * (inv * SCALE)).astype(BF16))
        return base + b + 1

    lax.fori_loop(0, NH, group, 0)

    def finish(b, carry):
        slot = jnp.bitwise_xor(slots[b], NH * turn[0])
        z = (slot % NH) * 2 + jnp.bitwise_xor(slot // NH, turn[2])

        def store(outs, z):
            for rel in range(NY):
                cut = slice(rel * ROWS, (rel + 1) * ROWS)
                outs[rel][z, :, :DH] = (acc[b, cut, :DH] * SCALE).astype(BF16)
                outs[rel][z, :, DH:] = acc[b, cut, DH:].astype(BF16)

        pl.when(z < NH)(lambda: store(lows, z))
        pl.when(z >= NH)(lambda: store(highs, z - NH))
        return carry

    lax.fori_loop(0, NZ, finish, 0)


VMEM = pl.BlockSpec(memory_space=pltpu.VMEM)
SMEM = pl.BlockSpec(memory_space=pltpu.SMEM)
ANY = pl.BlockSpec(memory_space=pl.ANY)
WIDE = jax.ShapeDtypeStruct((NH, ROWS, COLS), BF16)
NARROW = jax.ShapeDtypeStruct((NH, ROWS, 2 * DH), BF16)
WEIGHTS = jax.ShapeDtypeStruct((TILES, BLOCK, COLS), BF16)
STATS = jax.ShapeDtypeStruct((NH, 1, COLS), F32)
PARAMS = pltpu.CompilerParams(vmem_limit_bytes=62 * 1024 * 1024)


def cost(matmuls, exps):
    return pl.CostEstimate(
        flops=TILES * matmuls * 2 * BLOCK * COLS * DH * 2,
        bytes_accessed=24 * 1024 * 1024,
        transcendentals=exps * TILES * BLOCK * COLS,
    )


def run_forward(turn, q, pieces):
    return pl.pallas_call(
        forward,
        name="forward",
        out_shape=(WIDE, STATS, WEIGHTS),
        in_specs=[SMEM] + [VMEM] * 5,
        out_specs=[VMEM, VMEM, ANY],
        scratch_shapes=[
            pltpu.SMEM((NZ,), jnp.int32),
            pltpu.VMEM((NZ, BLOCK, COLS), F32),
            pltpu.VMEM((TILES, BLOCK, COLS), BF16),
            pltpu.VMEM((NZ, BLOCK, DH), BF16),
            pltpu.VMEM((NZ, DH, BLOCK), BF16),
            pltpu.VMEM((DH, COLS), F32),
            pltpu.SemaphoreType.DMA((TILES,)),
        ],
        compiler_params=PARAMS,
        cost_estimate=cost(2, 1),
    )(turn, q, *pieces)


def run_backward(turn, q, g, o, stat, pieces, weights):
    return pl.pallas_call(
        backward,
        name="backward",
        out_shape=(WIDE,) + (NARROW,) * (2 * NY),
        in_specs=[SMEM] + [VMEM] * 8 + [ANY],
        out_specs=[VMEM] * (1 + 2 * NY),
        scratch_shapes=[
            pltpu.SMEM((NZ,), jnp.int32),
            pltpu.VMEM((TILES, BLOCK, COLS), BF16),
            pltpu.VMEM((NZ, DH, BLOCK), BF16),
            pltpu.VMEM((NZ, BLOCK, DH), BF16),
            pltpu.VMEM((NZ, BLOCK, 2 * DH), F32),
            pltpu.VMEM((DH, COLS), F32),
            pltpu.SemaphoreType.DMA((TILES,)),
        ],
        compiler_params=PARAMS,
        cost_estimate=cost(4, 0),
    )(turn, q, g, o, stat, *pieces, weights)


def ring(step):
    return [(i, (i + step) % NY) for i in range(NY)]


def hop(x, step):
    return lax.ppermute(x, "zhi", [(i, (i + step) % NH) for i in range(NH)])


def swap(x):
    return lax.ppermute(x, "outer", [(0, 1), (1, 0)])


def exchange(x):
    return lax.all_to_all(x, "zhi", split_axis=0, concat_axis=0, tiled=True)


def after(x, *earlier):
    return lax.optimization_barrier((x, *earlier))[0]


def gather_y(kv):
    half = kv.shape[0] // 2
    up = lax.ppermute(kv, "y", ring(-1))
    down = lax.ppermute(kv, "y", ring(1))
    far = jnp.concatenate(
        [lax.ppermute(down[:half], "y", ring(1)), lax.ppermute(up[half:], "y", ring(-1))]
    )
    return kv, up, far, down


def add(x, y):
    return (x.astype(F32) + y.astype(F32)).astype(BF16)


def scatter_y(own, up, far, down):
    from_down = lax.ppermute(far[0], "y", ring(1))
    from_up = lax.ppermute(far[1], "y", ring(-1))
    up = (lax.ppermute(add(up[0], from_down), "y", ring(1)), lax.ppermute(up[1], "y", ring(1)))
    down = (
        lax.ppermute(down[0], "y", ring(-1)),
        lax.ppermute(add(down[1], from_up), "y", ring(-1)),
    )
    return jnp.concatenate(
        [
            (o.astype(F32) + (u.astype(F32) + d.astype(F32))).astype(BF16)
            for o, u, d in zip(own, up, down)
        ]
    )


def chunks(x):
    return x[0].reshape(ROWS, NH, COLS).transpose(1, 0, 2)


def rows(x):
    return x.transpose(1, 0, 2).reshape(1, ROWS, H * DH)


def shards(queries, keys, values, grad_out, positions):
    here = lax.axis_index("zhi").astype(jnp.int32)
    marks = jnp.concatenate([positions[0] // 64, positions[0] % 64]).astype(BF16)
    marks = jnp.broadcast_to(marks, (PADDED - ROWS, 2 * DH))
    own = lax.shift_right_logical(positions[0, 0], int(math.log2(2 * BLOCK)))
    own = jnp.where(here < NH // 2, own, NH - 1 - own).astype(jnp.int32)
    parts = []
    for step in range(NH):
        start = jnp.bitwise_and(here - step, NH - 1) * DH
        heads = [lax.dynamic_slice(x[0], (0, start), (ROWS, DH)) for x in (keys, values)]
        part = jnp.concatenate([jnp.concatenate(heads, axis=1), marks])
        parts.append(hop(part, -step) if step else part)
    kv = jnp.stack(parts)
    turn = jnp.stack([own, here, lax.axis_index("outer").astype(jnp.int32)])
    kv = jnp.concatenate([kv, swap(kv)])
    pieces = gather_y(kv)
    q, turn, _ = lax.optimization_barrier((chunks(queries), turn, kv))
    q = exchange(q)
    g = exchange(after(chunks(grad_out), q, *pieces))
    out, stat, weights = run_forward(turn, q, pieces)
    dq, *halves = run_backward(turn, q, g, out, stat, pieces, weights)
    out = exchange(out)
    dq = exchange(after(dq, out))
    dkv = after(scatter_y(*zip(halves[:NY], halves[NY:])), dq)
    dkv = lax.all_to_all(dkv, ("zhi", "outer"), split_axis=0, concat_axis=0, tiled=True)
    dkv = dkv.reshape(NH, 2, ROWS, 2 * DH)
    dkv = add(dkv[:, 0], dkv[:, 1])
    dk = jnp.concatenate([dkv[n, :, :DH] for n in range(KVH)], axis=1)[None]
    dv = jnp.concatenate([dkv[n, :, DH:] for n in range(KVH)], axis=1)[None]
    return rows(out), rows(dq), dk, dv


def solution(mesh):
    devices = mesh.devices.reshape(NH, NY, mesh.shape["inner"], mesh.shape["outer"])
    fine = Mesh(devices, ("zhi", "y", "inner", "outer"))
    wide = P("inner", ("zhi", "y", "outer"), None)
    return jax.shard_map(
        shards,
        mesh=fine,
        in_specs=(wide, wide, wide, wide, P("inner", ("zhi", "y", "outer"))),
        out_specs=(wide, wide, wide, wide),
        check_vma=False,
    )
```

```python
import math

import jax
import jax.numpy as jnp
from jax import lax
from jax.experimental import pallas as pl
from jax.experimental.pallas import tpu as pltpu
from jax.sharding import Mesh, PartitionSpec as P

H = 32
KVH = 4
DH = 128
ROWS = 128
PADDED = 144
BLOCK = 512
NY = 4
NH = 4
NZ = 2 * NH
PACK = H // NH
COLS = PACK * ROWS
TILES = NZ * (NZ + 1) // 4
NEGATIVE = -1e30
SCALE = 1.0 / math.sqrt(DH)
EXP2_SCALE = SCALE * math.log2(math.e)
DIMS_NT = (((1,), (1,)), ((), ()))
SLOTS = (0, 1, 4, 5, 6, 7, 2, 3)
F32 = jnp.float32
BF16 = jnp.bfloat16


def flip(ref, i):
    return jnp.concatenate([ref[i, :, k * DH : (k + 1) * DH].T for k in range(PACK)], axis=1)


def unflip(ref, i, value):
    for k in range(PACK):
        ref[i, :, k * DH : (k + 1) * DH] = value[:, k * ROWS : (k + 1) * ROWS].T


def twice(count, step, carry):
    carry = lax.fori_loop(
        0, count // 2, lambda j, c: step(2 * j + 1, step(2 * j, c)), carry
    )
    return lax.fori_loop(count // 2 * 2, count, step, carry)


def fold(x, op):
    return op(x.reshape(x.shape[0] // 8, 8, x.shape[1]), axis=0)


def own_block(turn, n):
    return jnp.where(n < NH // 2, n + 2 * turn[0], n + NH - 2 * turn[0])


def turned(turn, slot):
    return (slot // NH) * NH + jnp.bitwise_and(slot - turn[1], NH - 1)


def key_slot(turn, slots, b):
    return turned(turn, jnp.bitwise_xor(slots[b], NH * turn[0]))


def set_slots(slots):
    for b in range(NZ):
        slots[b] = SLOTS[b]


def forward(
    turn, q_ref, kv0, kv1, kv2, kv3, o_ref, stat_ref, p_hbm,
    slots, s_buf, p_buf, k_n, v_t, out_acc, sems,
):
    pieces = (kv0, kv1, kv2, kv3)
    set_slots(slots)

    def row_marks(piece, z):
        row = piece[z, ROWS : ROWS + 16, :].astype(F32)[0:1]
        return row[:, :DH] * 64.0 + row[:, DH:]

    def prepare(b, carry):
        z = key_slot(turn, slots, b)
        for rel in range(NY):
            cut = slice(rel * ROWS, (rel + 1) * ROWS)
            k_n[b, cut, :] = pieces[rel][z, :ROWS, :DH]
            v_t[b, :, cut] = pieces[rel][z, :ROWS, DH:].T
        return carry

    lax.fori_loop(0, NZ, prepare, 0)

    def group(i, base):
        b = own_block(turn, i)
        z = turned(turn, i)
        q_t = flip(q_ref, i)
        out_acc[...] = jnp.zeros((DH, COLS), F32)

        def first(j, top):
            s = jnp.dot(k_n[j], q_t, preferred_element_type=F32)
            s_buf[j] = s
            return jnp.maximum(top, fold(s, jnp.max))

        top = twice(b, first, jnp.full((8, COLS), NEGATIVE, F32))
        s = jnp.dot(k_n[b], q_t, preferred_element_type=F32)
        q_marks = jnp.broadcast_to(row_marks(kv0, z), (ROWS, ROWS))
        for rel in range(NY):
            cut = slice(rel * ROWS, (rel + 1) * ROWS)
            k_marks = jnp.broadcast_to(row_marks(pieces[rel], z), (ROWS, ROWS)).T
            seen = k_marks <= q_marks
            part = jnp.concatenate(
                [
                    jnp.where(seen, s[cut, k * ROWS : (k + 1) * ROWS], NEGATIVE)
                    for k in range(PACK)
                ],
                axis=1,
            )
            s_buf[b, cut, :] = part
            top = jnp.maximum(top, fold(part, jnp.max))
        top = jnp.max(top, axis=0, keepdims=True)

        def second(j, total):
            w = jnp.exp2((s_buf[j] - top) * EXP2_SCALE)
            total = total + fold(w, jnp.sum)
            w = w.astype(BF16)
            tile = base + j
            p_buf[tile] = w
            out_acc[...] += jnp.dot(v_t[j], w, preferred_element_type=F32)
            pltpu.make_async_copy(p_buf.at[tile], p_hbm.at[tile], sems.at[tile]).start()
            return total

        total = twice(b + 1, second, jnp.zeros((8, COLS), F32))
        inv = 1.0 / jnp.sum(total, axis=0, keepdims=True)
        unflip(o_ref, i, (out_acc[...] * inv).astype(BF16))
        stat_ref[i] = inv
        return base + b + 1

    lax.fori_loop(0, NH, group, 0)

    def wait(tile, carry):
        pltpu.make_async_copy(p_buf.at[tile], p_hbm.at[tile], sems.at[tile]).wait()
        return carry

    lax.fori_loop(0, TILES, wait, 0)


def backward(
    turn, q_ref, g_ref, o_ref, stat_ref, kv0, kv1, kv2, kv3, p_hbm,
    dq_ref, low0, low1, low2, low3, high0, high1, high2, high3,
    slots, p_buf, k_t, v_n, acc, dq_acc, sems,
):
    pieces = (kv0, kv1, kv2, kv3)
    lows = (low0, low1, low2, low3)
    highs = (high0, high1, high2, high3)
    set_slots(slots)

    def fetch(tile, carry):
        pltpu.make_async_copy(p_hbm.at[tile], p_buf.at[tile], sems.at[tile]).start()
        return carry

    lax.fori_loop(0, TILES, fetch, 0)

    def prepare(b, carry):
        z = key_slot(turn, slots, b)
        for rel in range(NY):
            cut = slice(rel * ROWS, (rel + 1) * ROWS)
            k_t[b, :, cut] = pieces[rel][z, :ROWS, :DH].T
            v_n[b, cut, :] = pieces[rel][z, :ROWS, DH:]
        acc[b] = jnp.zeros((BLOCK, 2 * DH), F32)
        return carry

    lax.fori_loop(0, NZ, prepare, 0)

    def group(i, base):
        b = own_block(turn, i)
        dq_acc[...] = jnp.zeros((DH, COLS), F32)
        q_t = flip(q_ref, i)
        g_t = flip(g_ref, i)
        o_t = flip(o_ref, i)
        inv = stat_ref[i]
        delta = jnp.sum(g_t.astype(F32) * o_t.astype(F32), axis=0, keepdims=True)
        q_n = (q_t.astype(F32) * inv).astype(BF16)
        g_n = (g_t.astype(F32) * inv).astype(BF16)

        def step(j, carry):
            tile = base + j
            pltpu.make_async_copy(p_hbm.at[tile], p_buf.at[tile], sems.at[tile]).wait()
            w = p_buf[tile]
            dp = jnp.dot(v_n[j], g_t, preferred_element_type=F32)
            ds = (w.astype(F32) * (dp - delta)).astype(BF16)
            acc[j, :, DH:] += lax.dot_general(w, g_n, DIMS_NT, preferred_element_type=F32)
            acc[j, :, :DH] += lax.dot_general(ds, q_n, DIMS_NT, preferred_element_type=F32)
            dq_acc[...] += jnp.dot(k_t[j], ds, preferred_element_type=F32)
            return carry

        twice(b + 1, step, 0)
        unflip(dq_ref, i, (dq_acc[...] * (inv * SCALE)).astype(BF16))
        return base + b + 1

    lax.fori_loop(0, NH, group, 0)

    def finish(b, carry):
        slot = jnp.bitwise_xor(slots[b], NH * turn[0])
        z = (slot % NH) * 2 + jnp.bitwise_xor(slot // NH, turn[2])

        def store(outs, z):
            for rel in range(NY):
                cut = slice(rel * ROWS, (rel + 1) * ROWS)
                outs[rel][z, :, :DH] = (acc[b, cut, :DH] * SCALE).astype(BF16)
                outs[rel][z, :, DH:] = acc[b, cut, DH:].astype(BF16)

        pl.when(z < NH)(lambda: store(lows, z))
        pl.when(z >= NH)(lambda: store(highs, z - NH))
        return carry

    lax.fori_loop(0, NZ, finish, 0)


VMEM = pl.BlockSpec(memory_space=pltpu.VMEM)
SMEM = pl.BlockSpec(memory_space=pltpu.SMEM)
ANY = pl.BlockSpec(memory_space=pl.ANY)
WIDE = jax.ShapeDtypeStruct((NH, ROWS, COLS), BF16)
NARROW = jax.ShapeDtypeStruct((NH, ROWS, 2 * DH), BF16)
WEIGHTS = jax.ShapeDtypeStruct((TILES, BLOCK, COLS), BF16)
STATS = jax.ShapeDtypeStruct((NH, 1, COLS), F32)
PARAMS = pltpu.CompilerParams(vmem_limit_bytes=63 * 1024 * 1024)


def cost(matmuls, exps):
    return pl.CostEstimate(
        flops=TILES * matmuls * 2 * BLOCK * COLS * DH * 2,
        bytes_accessed=24 * 1024 * 1024,
        transcendentals=exps * TILES * BLOCK * COLS,
    )


def run_forward(turn, q, pieces):
    return pl.pallas_call(
        forward,
        name="forward",
        out_shape=(WIDE, STATS, WEIGHTS),
        in_specs=[SMEM] + [VMEM] * 5,
        out_specs=[VMEM, VMEM, ANY],
        scratch_shapes=[
            pltpu.SMEM((NZ,), jnp.int32),
            pltpu.VMEM((NZ, BLOCK, COLS), F32),
            pltpu.VMEM((TILES, BLOCK, COLS), BF16),
            pltpu.VMEM((NZ, BLOCK, DH), BF16),
            pltpu.VMEM((NZ, DH, BLOCK), BF16),
            pltpu.VMEM((DH, COLS), F32),
            pltpu.SemaphoreType.DMA((TILES,)),
        ],
        compiler_params=PARAMS,
        cost_estimate=cost(2, 1),
    )(turn, q, *pieces)


def run_backward(turn, q, g, o, stat, pieces, weights):
    return pl.pallas_call(
        backward,
        name="backward",
        out_shape=(WIDE,) + (NARROW,) * (2 * NY),
        in_specs=[SMEM] + [VMEM] * 8 + [ANY],
        out_specs=[VMEM] * (1 + 2 * NY),
        scratch_shapes=[
            pltpu.SMEM((NZ,), jnp.int32),
            pltpu.VMEM((TILES, BLOCK, COLS), BF16),
            pltpu.VMEM((NZ, DH, BLOCK), BF16),
            pltpu.VMEM((NZ, BLOCK, DH), BF16),
            pltpu.VMEM((NZ, BLOCK, 2 * DH), F32),
            pltpu.VMEM((DH, COLS), F32),
            pltpu.SemaphoreType.DMA((TILES,)),
        ],
        compiler_params=PARAMS,
        cost_estimate=cost(4, 0),
    )(turn, q, g, o, stat, *pieces, weights)


def ring(step):
    return [(i, (i + step) % NY) for i in range(NY)]


def hop(x, step):
    return lax.ppermute(x, "zhi", [(i, (i + step) % NH) for i in range(NH)])


def swap(x):
    return lax.ppermute(x, "outer", [(0, 1), (1, 0)])


def exchange(x):
    return lax.all_to_all(x, "zhi", split_axis=0, concat_axis=0, tiled=True)


def after(x, *earlier):
    return lax.optimization_barrier((x, *earlier))[0]


def gather_y(kv):
    half = kv.shape[0] // 2
    up = lax.ppermute(kv, "y", ring(-1))
    down = lax.ppermute(kv, "y", ring(1))
    far = jnp.concatenate(
        [lax.ppermute(down[:half], "y", ring(1)), lax.ppermute(up[half:], "y", ring(-1))]
    )
    return kv, up, far, down


def add(x, y):
    return (x.astype(F32) + y.astype(F32)).astype(BF16)


def scatter_y(own, up, far, down):
    from_down = lax.ppermute(far[0], "y", ring(1))
    from_up = lax.ppermute(far[1], "y", ring(-1))
    up = (lax.ppermute(add(up[0], from_down), "y", ring(1)), lax.ppermute(up[1], "y", ring(1)))
    down = (
        lax.ppermute(down[0], "y", ring(-1)),
        lax.ppermute(add(down[1], from_up), "y", ring(-1)),
    )
    return jnp.concatenate(
        [
            (o.astype(F32) + (u.astype(F32) + d.astype(F32))).astype(BF16)
            for o, u, d in zip(own, up, down)
        ]
    )


def chunks(x):
    return x[0].reshape(ROWS, NH, COLS).transpose(1, 0, 2)


def rows(x):
    return x.transpose(1, 0, 2).reshape(1, ROWS, H * DH)


def shards(queries, keys, values, grad_out, positions):
    here = lax.axis_index("zhi").astype(jnp.int32)
    marks = jnp.concatenate(
        [lax.shift_right_logical(positions[0], 6), jnp.bitwise_and(positions[0], 63)]
    ).astype(BF16)
    marks = jnp.broadcast_to(marks, (PADDED - ROWS, 2 * DH))
    own = lax.shift_right_logical(positions[0, 0], int(math.log2(2 * BLOCK)))
    own = jnp.where(here < NH // 2, own, NH - 1 - own).astype(jnp.int32)
    parts = []
    for step in range(NH):
        start = jnp.bitwise_and(here - step, NH - 1) * DH
        heads = [lax.dynamic_slice(x[0], (0, start), (ROWS, DH)) for x in (keys, values)]
        part = jnp.concatenate([jnp.concatenate(heads, axis=1), marks])
        parts.append(hop(part, -step) if step else part)
    kv = jnp.stack(parts)
    turn = jnp.stack([own, here, lax.axis_index("outer").astype(jnp.int32)])
    kv = jnp.concatenate([kv, swap(kv)])
    pieces = gather_y(kv)
    q, turn, _ = lax.optimization_barrier((chunks(queries), turn, kv))
    q = exchange(q)
    g = exchange(after(chunks(grad_out), q, *pieces))
    out, stat, weights = run_forward(turn, q, pieces)
    dq, *halves = run_backward(turn, q, g, out, stat, pieces, weights)
    out = exchange(out)
    dq = exchange(after(dq, out))
    dkv = after(scatter_y(*zip(halves[:NY], halves[NY:])), dq)
    dkv = lax.all_to_all(dkv, ("zhi", "outer"), split_axis=0, concat_axis=0, tiled=True)
    dkv = dkv.reshape(NH, 2, ROWS, 2 * DH)
    dkv = add(dkv[:, 0], dkv[:, 1])
    dk = jnp.concatenate([dkv[n, :, :DH] for n in range(KVH)], axis=1)[None]
    dv = jnp.concatenate([dkv[n, :, DH:] for n in range(KVH)], axis=1)[None]
    return rows(out), rows(dq), dk, dv


def solution(mesh):
    devices = mesh.devices.reshape(NH, NY, mesh.shape["inner"], mesh.shape["outer"])
    fine = Mesh(devices, ("zhi", "y", "inner", "outer"))
    wide = P("inner", ("zhi", "y", "outer"), None)
    return jax.shard_map(
        shards,
        mesh=fine,
        in_specs=(wide, wide, wide, wide, P("inner", ("zhi", "y", "outer"))),
        out_specs=(wide, wide, wide, wide),
        check_vma=False,
    )
```
